32 devices in a mesh: groups: 2 (over x), wide: 16 (over z, y, core).
Axes of the slice: x: 2, y: 2, z: 4, core: 2. Of those that a mesh axis runs over, the one named last changes fastest.
Arguments:
- tokens: bfloat16 [2, 64, 18432], P(None, 'groups', 'wide'), parts along dimension 1, may hold values from -360 to 360
- norm_gain: float32 [18432], replicated, may hold values from 0.1 to 1.9
- w_qkv: bfloat16 [18432, 12800], P(None, 'wide'), may hold values from -0.046875 to 0.046875
- w_out: bfloat16 [12288, 18432], P(None, 'wide'), may hold values from -0.0546875 to 0.0546875
- cache_k: bfloat16 [64, 2048, 256], P(('groups', 'wide')), parts along dimension 0, may hold values from -6 to 6
- cache_v: bfloat16 [64, 2048, 256], P(('groups', 'wide')), parts along dimension 0, may hold values from -6 to 6
- lengths: int32 [64], P(('groups', 'wide')), parts along dimension 0, may hold values from 1 to 2048, as said below
Outputs:
- attended: bfloat16 [2, 64, 18432], P(None, 'groups', 'wide'), parts along dimension 1
The draws below stay inside these ranges and needn't reach their ends.
There are 2 independent parts, one for each index of `groups`. The reference program is written for one: setup_inputs(seed, part) draws one part's arguments, and reference() takes and returns one part's arrays. A program takes and returns all parts, laid end to end along the dimension named above; an argument that names none is the same for every part. Nothing has to cross between parts.
Inputs may be any that keep to these rules, and one draw needn't show every extreme that they name: Sequence b uses cache slots 0 to lengths[b] - 1; some sequence has 2048.
All inputs are finite; a program needn't handle non-finite values.
Results may differ from the reference program's by a relative error of at most 0.01.
Values may be sent and summed in bfloat16 or wider, within the bound.
A program may use at most 128 MiB of HBM per device.

```python
import math
import jax
import jax.numpy as jnp
from jax import lax

D = 18432
HEADS = 48
HD = 256
LCACHE = 2048
STEPS = 2
B = 32


def draw_tokens(key, part):
    key = jax.random.fold_in(key, 11)
    key_base, key_column, key_row = jax.random.split(key, 3)
    column = jnp.arange(D, dtype=jnp.float32)
    column_scale = 3.0 ** (column / (D - 1)) * jnp.exp(jax.random.uniform(key_column, (D,), jnp.float32, 0.0, math.log(3.0)))
    row_scale = jnp.exp(jax.random.uniform(key_row, (STEPS, B, 1), jnp.float32, 0.0, math.log(10.0)))
    base = jnp.clip(jax.random.normal(key_base, (STEPS, B, D), jnp.float32), -4.0, 4.0)
    return (base * column_scale * row_scale).astype(jnp.bfloat16)


def draw_lengths(key, part):
    key = jax.random.fold_in(key, 23)
    key_values, key_pick = jax.random.split(key)
    values = jax.random.randint(key_values, (B,), 1, LCACHE + 1, dtype=jnp.int32)
    picked = jax.random.randint(key_pick, (), 0, B, dtype=jnp.int32)
    return jnp.where(jnp.arange(B, dtype=jnp.int32) == picked, LCACHE, values).astype(jnp.int32)


def shard_levels(own_key, dims, shards, low, high):
    def one(axis_at, blocks):
        draws = jax.random.uniform(jax.random.fold_in(jax.random.fold_in(own_key, 6), axis_at), (blocks,), jnp.float32, low / len(shards), high / len(shards))
        return jnp.repeat(jnp.exp(draws), dims[axis_at] // blocks).reshape((-1,) + (1,) * (len(dims) - axis_at - 1))

    level = one(*shards[0])
    for cut in shards[1:]:
        level = level * one(*cut)
    return level


def bell_draw(key, shape, scale, reach, cuts=(), held_as=jnp.bfloat16):
    entries = jax.random.normal(key, shape, jnp.float32) * scale
    if len(cuts) > 0:
        entries = shard_levels(key, shape, cuts, -0.22, 0.18) * entries
    return jnp.clip(entries, min=-reach, max=reach).astype(held_as)


def setup_inputs(seed: int = 0, part: int = 0) -> dict:
    splits = jax.random.split(jax.random.key(seed), 8)
    part_splits = jax.random.split(jax.random.fold_in(splits[7], part), 8)
    return {
        "tokens": draw_tokens(jax.random.fold_in(jax.random.fold_in(splits[7], part), 71), part),
        "norm_gain": jnp.clip(1.0 + 0.18 * jax.random.normal(splits[1], (D,), jnp.float32), 0.1, 1.9),
        "w_qkv": bell_draw(splits[2], (D, (HEADS + 2) * HD), D ** -0.5, 0.046875, ((1, 16),)),
        "w_out": bell_draw(splits[3], (HEADS * HD, D), (HEADS * HD) ** -0.5, 0.0546875, ((1, 16),)),
        "cache_k": bell_draw(part_splits[4], (B, LCACHE, HD), 1.0, 6.0, ((0, 16),)),
        "cache_v": bell_draw(part_splits[5], (B, LCACHE, HD), 1.0, 6.0, ((0, 16),)),
        "lengths": draw_lengths(jax.random.fold_in(jax.random.fold_in(splits[7], part), 71), part),
    }


norm_eps = 1e-05

def rotate(values, cosine, sine_table):
    half = values.shape[-1] // 2
    first = values[..., :half]
    second = values[..., half:]
    return jnp.concatenate([first * cosine - second * sine_table, second * cosine + first * sine_table], axis=-1)

def attend(projected, cache_k, cache_v, lengths, heads, head_dim):
    step_count, seq_rows, _ = projected.shape
    width_q = heads * head_dim
    query = projected[..., :width_q].astype(jnp.float32).reshape(step_count, seq_rows, heads, head_dim)
    key_new = projected[..., width_q:width_q + head_dim].astype(jnp.float32)
    value_new = projected[..., width_q + head_dim:].astype(jnp.float32)
    positions = lengths[None, :] + jnp.arange(step_count, dtype=jnp.int32)[:, None]
    half = head_dim // 2
    freqs = jnp.exp(jnp.arange(half, dtype=jnp.float32) * (-2.0 * math.log(10000.0) / head_dim))
    angles = positions.astype(jnp.float32)[..., None] * freqs
    cosine = jnp.cos(angles)
    sine_table = jnp.sin(angles)
    query = rotate(query, cosine[:, :, None, :], sine_table[:, :, None, :]).astype(jnp.bfloat16).astype(jnp.float32)
    key_new = rotate(key_new, cosine, sine_table).astype(jnp.bfloat16).astype(jnp.float32)
    scale = 1.0 / math.sqrt(head_dim)
    cache_scores = jnp.einsum('snhd,nld->snhl', query, cache_k.astype(jnp.float32)) * scale
    slots = jnp.arange(cache_k.shape[1], dtype=jnp.int32)
    valid = slots[None, :] < lengths[:, None]
    cache_scores = jnp.where(valid[None, :, None, :], cache_scores, -1e+30)
    new_scores = jnp.einsum('snhd,tnd->snht', query, key_new) * scale
    order = jnp.arange(step_count, dtype=jnp.int32)
    causal = order[None, :] <= order[:, None]
    new_scores = jnp.where(causal[:, None, None, :], new_scores, -1e+30)
    top = jnp.maximum(lax.optimization_barrier(jnp.max(cache_scores, axis=-1)), lax.optimization_barrier(jnp.max(new_scores, axis=-1)))
    exp_cache = jnp.exp(cache_scores - top[..., None])
    exp_new = jnp.exp(new_scores - top[..., None])
    denom = lax.optimization_barrier(jnp.sum(exp_cache, axis=-1)) + lax.optimization_barrier(jnp.sum(exp_new, axis=-1))
    w_cache = (exp_cache / denom[..., None]).astype(jnp.bfloat16).astype(jnp.float32)
    w_new = (exp_new / denom[..., None]).astype(jnp.bfloat16).astype(jnp.float32)
    mixed = jnp.einsum('snhl,nld->snhd', w_cache, cache_v.astype(jnp.float32)) + jnp.einsum('snht,tnd->snhd', w_new, value_new)
    return mixed.reshape(step_count, seq_rows, width_q).astype(jnp.bfloat16)

def reference(tokens, norm_gain, w_qkv, w_out, cache_k, cache_v, lengths):
    widened = tokens.astype(jnp.float32)
    center = lax.optimization_barrier(jnp.mean(widened, axis=-1, keepdims=True))
    spread = lax.optimization_barrier(jnp.mean(widened * widened, axis=-1, keepdims=True)) - center * center
    normed = ((widened - center) * jax.lax.rsqrt(spread + norm_eps) * norm_gain).astype(jnp.bfloat16)
    columns = w_qkv.shape[1]
    projected = jnp.dot(normed.reshape(STEPS * B, D), w_qkv, preferred_element_type=jnp.float32)
    projected = projected.astype(jnp.bfloat16).reshape(STEPS, B, columns)
    mixed = attend(projected, cache_k, cache_v, lengths, HEADS, HD)
    result = jnp.dot(mixed.reshape(STEPS * B, HEADS * HD), w_out, preferred_element_type=jnp.float32)
    return result.astype(jnp.bfloat16).reshape(STEPS, B, D)
```

```python
import functools
import math

import jax
import jax.numpy as jnp
from jax import lax
from jax.experimental import pallas as pl
from jax.experimental.pallas import tpu as pltpu
from jax.sharding import PartitionSpec as P

norm_eps = 1e-05
MESH = pl.DeviceIdType.MESH
Z, Y, C = 4, 2, 2
WIDE = Z * Y * C
SLOTS = 8
PIECES = 4
GROUP = 4


def rotate(values, cosine, sine_table):
    half = values.shape[-1] // 2
    first = values[..., :half]
    second = values[..., half:]
    return jnp.concatenate(
        [first * cosine - second * sine_table, second * cosine + first * sine_table], axis=-1
    )


def attend(projected, cache_k, cache_v, lengths, heads, head_dim):
    step_count, seq_rows, _ = projected.shape
    width_q = heads * head_dim
    query = (
        projected[..., :width_q].astype(jnp.float32).reshape(step_count, seq_rows, heads, head_dim)
    )
    key_new = projected[..., width_q : width_q + head_dim].astype(jnp.float32)
    value_new = projected[..., width_q + head_dim :]
    positions = lengths[None, :] + jnp.arange(step_count, dtype=jnp.int32)[:, None]
    half = head_dim // 2
    freqs = jnp.exp(jnp.arange(half, dtype=jnp.float32) * (-2.0 * math.log(10000.0) / head_dim))
    angles = positions.astype(jnp.float32)[..., None] * freqs
    cosine = jnp.cos(angles)
    sine_table = jnp.sin(angles)
    query = rotate(query, cosine[:, :, None, :], sine_table[:, :, None, :]).astype(jnp.bfloat16)
    key_new = rotate(key_new, cosine, sine_table).astype(jnp.bfloat16)
    scale = 1.0 / math.sqrt(head_dim)
    cache_scores = (
        jnp.einsum("snhd,nld->snhl", query, cache_k, preferred_element_type=jnp.float32) * scale
    )
    slots = jnp.arange(cache_k.shape[1], dtype=jnp.int32)
    valid = slots[None, :] < lengths[:, None]
    cache_scores = jnp.where(valid[None, :, None, :], cache_scores, -1e30)
    new_scores = (
        jnp.einsum("snhd,tnd->snht", query, key_new, preferred_element_type=jnp.float32) * scale
    )
    order = jnp.arange(step_count, dtype=jnp.int32)
    causal = order[None, :] <= order[:, None]
    new_scores = jnp.where(causal[:, None, None, :], new_scores, -1e30)
    top = jnp.maximum(jnp.max(cache_scores, axis=-1), jnp.max(new_scores, axis=-1))
    exp_cache = jnp.exp(cache_scores - top[..., None])
    exp_new = jnp.exp(new_scores - top[..., None])
    denom = jnp.sum(exp_cache, axis=-1) + jnp.sum(exp_new, axis=-1)
    w_cache = (exp_cache / denom[..., None]).astype(jnp.bfloat16)
    w_new = (exp_new / denom[..., None]).astype(jnp.bfloat16)
    mixed = jnp.einsum("snhl,nld->snhd", w_cache, cache_v, preferred_element_type=jnp.float32)
    mixed = mixed + jnp.einsum(
        "snht,tnd->snhd", w_new, value_new, preferred_element_type=jnp.float32
    )
    return mixed.reshape(step_count, seq_rows, width_q).astype(jnp.bfloat16)


def on_device(tokens, norm_gain, w_qkv, w_out, cache_k, cache_v, lengths):
    gathered = lax.all_gather(tokens, "wide", axis=2, tiled=True)
    widened = gathered.astype(jnp.float32)
    center = jnp.mean(widened, axis=-1, keepdims=True)
    spread = jnp.mean(widened * widened, axis=-1, keepdims=True) - center * center
    normed = ((widened - center) * lax.rsqrt(spread + norm_eps) * norm_gain).astype(jnp.bfloat16)
    projected = jnp.einsum("sbd,dc->sbc", normed, w_qkv, preferred_element_type=jnp.float32)
    projected = projected.astype(jnp.bfloat16)
    per_sequence = lax.all_to_all(projected, "wide", split_axis=1, concat_axis=2, tiled=True)
    head_dim = cache_k.shape[2]
    heads = per_sequence.shape[2] // head_dim - 2
    mixed = attend(per_sequence, cache_k, cache_v, lengths, heads, head_dim)
    result = jnp.einsum(
        "snh,hd->snd",
        lax.all_gather(mixed, "wide", axis=1, tiled=True),
        w_out,
        preferred_element_type=jnp.float32,
    )
    return result.astype(jnp.bfloat16)


def iota(shape, axis):
    return lax.broadcasted_iota(jnp.int32, shape, axis)


def pick(mask):
    return jnp.where(mask, 1.0, 0.0).astype(jnp.bfloat16)


def dot(a, b):
    return jnp.dot(a, b, preferred_element_type=jnp.float32)


def dot_t(a, b):
    return lax.dot_general(a, b, (((1,), (1,)), ((), ())), preferred_element_type=jnp.float32)


def fused_kernel(
    lengths,
    tokens,
    gain,
    cos_ref,
    sin_ref,
    w_qkv,
    w_out,
    cache_k,
    cache_v,
    out,
    shards,
    stats,
    w_in,
    w_last,
    keys,
    values,
    acc,
    to_send,
    arrived,
    gathered,
    total,
    columns,
    local_sem,
    last_sem,
    cache_sem,
    stat_send,
    stat_recv,
    send_z,
    send_y,
    send_c,
    recv1,
    all_send,
    all_recv,
    send2_z,
    send2_y,
    send2_c,
    recv2,
):
    me = lax.axis_index("wide")
    z = me // (Y * C)
    y = (me // C) % Y
    c = me % C
    depth = tokens.shape[1]
    rows = tokens.shape[0]
    seqs = rows // 2
    out_depth = w_last.shape[1]
    width = w_qkv.shape[1]
    heads = w_out.shape[0] // 256
    groups = heads // GROUP
    mirrored = (z + z // 2) % 2
    upper = z // 2

    def z_at(p):
        m = p + mirrored * (1 - 2 * p) * (1 - p // 2)
        return m + upper * (3 - 2 * m)

    def index(zz, yy, cc):
        return (zz * Y + yy) * C + cc

    def remote(src, dst, send_sem, recv_sem, target):
        return pltpu.make_async_remote_copy(
            src_ref=src,
            dst_ref=dst,
            send_sem=send_sem,
            recv_sem=recv_sem,
            device_id={"wide": target},
            device_id_type=MESH,
        )

    y_peer = index(z, 1 - y, c)
    c_peer = index(z, y, 1 - c)

    def load_in(owner):
        return pltpu.make_async_copy(
            w_qkv.at[pl.ds(pl.multiple_of(owner * depth, depth), depth)],
            w_in.at[owner],
            local_sem.at[owner],
        )

    def load_last(g):
        return pltpu.make_async_copy(
            w_out.at[pl.ds(pl.multiple_of(g * out_depth, out_depth), out_depth)],
            w_last.at[g % SLOTS],
            last_sem.at[g],
        )

    load_keys = pltpu.make_async_copy(cache_k, keys, cache_sem.at[0])
    load_values = pltpu.make_async_copy(cache_v, values, cache_sem.at[1])

    def load_round(p, carry):
        @pl.when(p <= 3)
        def _():
            load_in(index(z_at(p), y, c)).start()
            load_in(index(z_at(p), y, 1 - c)).start()

        @pl.when(p >= 1)
        def _():
            load_in(index(z_at(p - 1), 1 - y, c)).start()
            load_in(index(z_at(p - 1), 1 - y, 1 - c)).start()

        return carry

    lax.fori_loop(0, 5, load_round, 0)

    barrier = pltpu.get_barrier_semaphore()

    def greet(k, carry):
        pl.semaphore_signal(
            barrier, inc=1, device_id={"wide": (me + k) % WIDE}, device_id_type=MESH
        )
        return carry

    lax.fori_loop(1, WIDE, greet, 0)

    widened = tokens[...].astype(jnp.float32)
    diagonal = iota((rows, 128), 0) == iota((rows, 128), 1)

    def as_row(column):
        return jnp.sum(jnp.where(diagonal, column, 0.0), axis=0, keepdims=True)

    def as_column(row):
        return jnp.sum(jnp.where(diagonal, row, 0.0), axis=1, keepdims=True)

    sums = as_row(jnp.sum(widened, axis=1, keepdims=True))
    squares = as_row(jnp.sum(widened * widened, axis=1, keepdims=True))
    line = iota((8, 128), 0)
    stats[me] = jnp.where(line == 0, sums, jnp.where(line == 1, squares, 0.0))

    pl.semaphore_wait(barrier, WIDE - 1)

    def stat_copy(k):
        return remote(
            stats.at[me], stats.at[me], stat_send.at[k], stat_recv.at[me], (me + k) % WIDE
        )

    def stat_start(k, carry):
        stat_copy(k).start()
        return carry

    lax.fori_loop(1, WIDE, stat_start, 0)

    def own_copy(send_sem, target):
        return remote(tokens, shards.at[me], send_sem, recv1.at[me], target)

    @pl.when(z < Z - 1)
    def _():
        own_copy(send_z.at[0], index(z + 1, y, c)).start()

    @pl.when(z > 0)
    def _():
        own_copy(send_z.at[1], index(z - 1, y, c)).start()

    own_copy(send_y.at[0], y_peer).start()
    own_copy(send_c.at[0], c_peer).start()

    def shard_copy(owner, send_sem, target):
        return remote(shards.at[owner], shards.at[owner], send_sem, recv1.at[owner], target)

    def next_z(zz):
        return z + jnp.where(zz > z, -1, 1)

    def can_go(zz):
        after = next_z(zz)
        return jnp.logical_and(after >= 0, after < Z)

    def arrival(owner):
        shard_copy(owner, send_z.at[0], c_peer).wait_recv()

    shards[me] = tokens[...]
    acc[...] = jnp.zeros_like(acc)

    def stat_wait(k, carry):
        j = (me + k) % WIDE
        remote(stats.at[j], stats.at[j], stat_send.at[k], stat_recv.at[j], j).wait_recv()
        return carry

    lax.fori_loop(1, WIDE, stat_wait, 0)
    whole = jnp.sum(stats[...], axis=0)
    features = float(depth * WIDE)
    center = as_column(whole[0:1]) / features
    spread = as_column(whole[1:2]) / features - center * center
    columns[0] = jnp.broadcast_to(center, (rows, 128))
    columns[1] = jnp.broadcast_to(lax.rsqrt(spread + norm_eps), (rows, 128))

    def project(owner):
        load_in(owner).wait()
        x = shards[owner].astype(jnp.float32)
        normed = (x - columns[0][:, 0:1]) * columns[1][:, 0:1] * gain[owner]
        acc[:, 0:width] += dot(normed.astype(jnp.bfloat16), w_in[owner])

    def round1(p, carry):
        @pl.when(jnp.logical_and(p >= 1, p <= 3))
        def _():
            zz = z_at(p)
            owner = index(zz, y, c)
            arrival(owner)

            @pl.when(can_go(zz))
            def _():
                shard_copy(owner, send_z.at[1 + p], index(next_z(zz), y, c)).start()

            shard_copy(owner, send_y.at[p], y_peer).start()
            shard_copy(owner, send_c.at[p], c_peer).start()

        @pl.when(p >= 1)
        def _():
            owner = index(z_at(p - 1), 1 - y, c)
            arrival(owner)
            shard_copy(owner, send_c.at[3 + p], c_peer).start()

        @pl.when(p == 2)
        def _():
            load_keys.start()
            load_values.start()

            def body(g, inner):
                load_last(g).start()
                return inner

            lax.fori_loop(0, SLOTS, body, 0)

        def part(i, inner):
            late = i // 2
            zz = z_at(p - late)

            @pl.when(jnp.logical_and(p - late >= 0, p - late <= 3))
            def _():
                owner = index(zz, (y + late) % Y, (c + i) % C)

                @pl.when(i % 2 == 1)
                def _():
                    arrival(owner)

                project(owner)

            return inner

        return lax.fori_loop(0, 4, part, carry)

    lax.fori_loop(0, 5, round1, 0)

    offset = (width * me) % 256
    shifted = pltpu.roll(acc[...], offset, 1).astype(jnp.bfloat16)
    row = iota((WIDE * 16, rows), 0)
    token = ((row >> 1) & 1) * seqs + 2 * (row >> 4) + (row & 1)
    chosen = iota((WIDE * 16, rows), 1) == token
    sending = jnp.zeros((WIDE * 16, 256), jnp.float32)
    for hh in range(GROUP):
        sending += dot(
            pick(jnp.logical_and(chosen, ((row >> 2) & 3) == hh)),
            shifted[:, hh * 256 : (hh + 1) * 256],
        )
    to_send[...] = sending.astype(jnp.bfloat16).reshape(to_send.shape)

    def all_copy(k):
        t = (me + k) % WIDE
        return remote(to_send.at[t], arrived.at[me], all_send.at[k], all_recv.at[me], t)

    def all_start(k, carry):
        all_copy(k).start()
        return carry

    lax.fori_loop(1, WIDE, all_start, 0)
    arrived[me] = to_send[me]
    load_keys.wait()
    load_values.wait()

    def all_wait(k, carry):
        j = (me + k) % WIDE
        remote(to_send.at[j], arrived.at[j], all_send.at[k], all_recv.at[j], j).wait_recv()
        return carry

    lax.fori_loop(1, WIDE, all_wait, 0)

    blocks = arrived[...].reshape(WIDE * 16, 256)
    query_rows = 2 * heads
    col = iota((query_rows + 16, WIDE * 16), 1)
    head = ((width * (col >> 4)) >> 8) + ((col >> 2) & 3)
    step = (col >> 1) & 1
    target = jnp.where(
        head < heads, step * heads + head, query_rows + 8 * (head - heads) + step
    )
    placed = iota((query_rows + 16, WIDE * 16), 0) == target
    scale = 1.0 / math.sqrt(256)
    slots = keys.shape[1]
    sending = jnp.zeros((4 * heads, 256), jnp.float32)
    for n in range(2):
        mine = dot(pick(jnp.logical_and(placed, (col & 1) == n)), blocks)

        def turn(block, cosine, sine_table):
            first, second = block[:, 0:128], block[:, 128:256]
            return jnp.concatenate(
                [first * cosine - second * sine_table, second * cosine + first * sine_table],
                axis=1,
            ).astype(jnp.bfloat16)

        def by_step(table, count, half):
            at = iota((count, 128), 0)
            return jnp.where(at < half, table[n : n + 1, :], table[n + 2 : n + 3, :])

        query = turn(
            mine[0:query_rows],
            by_step(cos_ref, query_rows, heads),
            by_step(sin_ref, query_rows, heads),
        )
        key_new = turn(
            mine[query_rows : query_rows + 8], by_step(cos_ref, 8, 1), by_step(sin_ref, 8, 1)
        )
        value_new = mine[query_rows + 8 : query_rows + 16].astype(jnp.bfloat16)
        scores = dot_t(query, keys[n]) * scale
        scores = jnp.where(iota((query_rows, slots), 1) < lengths[n], scores, -1e30)
        fresh = dot_t(query, key_new) * scale
        t = iota((query_rows, 8), 1)
        s = jnp.where(iota((query_rows, 8), 0) >= heads, 1, 0)
        fresh = jnp.where(t <= s, fresh, -1e30)
        top = jnp.maximum(
            jnp.max(scores, axis=1, keepdims=True), jnp.max(fresh, axis=1, keepdims=True)
        )
        scores = jnp.exp(scores - top)
        fresh = jnp.exp(fresh - top)
        denom = jnp.sum(scores, axis=1, keepdims=True) + jnp.sum(fresh, axis=1, keepdims=True)
        inverse = 1.0 / denom
        mixed = dot((scores * inverse).astype(jnp.bfloat16), values[n])
        mixed += dot((fresh * inverse).astype(jnp.bfloat16), value_new)
        at = iota((4 * heads, query_rows), 0)
        from_row = ((at >> 1) & 1) * heads + (at >> 2)
        sending += dot(
            pick(
                jnp.logical_and(
                    iota((4 * heads, query_rows), 1) == from_row, (at & 1) == n
                )
            ),
            mixed.astype(jnp.bfloat16),
        )
    gathered[me] = sending.astype(jnp.bfloat16)

    high = gathered.shape[1] // PIECES

    def piece_copy(owner, q, send_sem, target):
        part = gathered.at[owner, pl.ds(pl.multiple_of(q * high, high), high)]
        return remote(part, part, send_sem, recv2.at[q, owner], target)

    def piece_start(q, carry):
        @pl.when(z < Z - 1)
        def _():
            piece_copy(me, q, send2_z.at[q, 0], index(z + 1, y, c)).start()

        @pl.when(z > 0)
        def _():
            piece_copy(me, q, send2_z.at[q, 1], index(z - 1, y, c)).start()

        piece_copy(me, q, send2_y.at[q, 0], y_peer).start()
        piece_copy(me, q, send2_c.at[q, 0], c_peer).start()
        return carry

    lax.fori_loop(0, PIECES, piece_start, 0)

    def piece_arrival(owner, q):
        piece_copy(owner, q, send2_z.at[q, 0], c_peer).wait_recv()

    def forward(q, p):
        @pl.when(p <= 3)
        def _():
            zz = z_at(p)
            owner = index(zz, y, c)
            piece_arrival(owner, q)

            @pl.when(can_go(zz))
            def _():
                piece_copy(owner, q, send2_z.at[q, 1 + p], index(next_z(zz), y, c)).start()

            piece_copy(owner, q, send2_y.at[q, p], y_peer).start()
            piece_copy(owner, q, send2_c.at[q, p], c_peer).start()

        owner = index(z_at(p - 1), 1 - y, c)
        piece_arrival(owner, q)
        piece_copy(owner, q, send2_c.at[q, 3 + p], c_peer).start()

        @pl.when(p == 4)
        def _():
            def body(j, inner):
                piece_arrival(index(z_at(j // 2), (y + j) % Y, 1 - c), q)
                return inner

            lax.fori_loop(0, 8, body, 0)

    def forward_loop(p, carry):
        forward(0, p)
        return carry

    lax.fori_loop(1, 5, forward_loop, 0)

    total[...] = jnp.zeros_like(total)
    per_piece = groups // PIECES
    i = iota((rows * GROUP, WIDE * 16), 0)
    m = i % rows
    b = m % seqs
    source = (b >> 1) * 16 + (i // rows) * 4 + (m // seqs) * 2 + (b & 1)
    reorder = pick(iota((rows * GROUP, WIDE * 16), 1) == source)

    def multiply(g, carry):
        q = g // per_piece
        r = g % per_piece

        @pl.when(q < PIECES - 1)
        def _():
            def body(p, inner):
                forward(q + 1, p)
                return inner

            lax.fori_loop(
                1 + (4 * r) // per_piece, 1 + (4 * r + 4) // per_piece, body, 0
            )

        load_last(g).wait()
        block = gathered[:, pl.ds(pl.multiple_of(g * 16, 16), 16), :].reshape(WIDE * 16, 256)
        ordered = dot(reorder, block).astype(jnp.bfloat16)
        lined = jnp.concatenate(
            [ordered[h * rows : (h + 1) * rows] for h in range(GROUP)], axis=1
        )
        total[...] += dot(lined, w_last[g % SLOTS])

        @pl.when(g + SLOTS < groups)
        def _():
            load_last(g + SLOTS).start()

        return carry

    lax.fori_loop(0, groups, multiply, 0)
    out[...] = total[...].astype(jnp.bfloat16)

    def sent(k, carry):
        stat_copy(k).wait_send()
        all_copy(k).wait_send()
        return carry

    lax.fori_loop(1, WIDE, sent, 0)

    @pl.when(z < Z - 1)
    def _():
        own_copy(send_z.at[0], index(z + 1, y, c)).wait_send()

    @pl.when(z > 0)
    def _():
        own_copy(send_z.at[1], index(z - 1, y, c)).wait_send()

    own_copy(send_y.at[0], y_peer).wait_send()
    own_copy(send_c.at[0], c_peer).wait_send()

    def sent1(p, carry):
        @pl.when(p <= 3)
        def _():
            zz = z_at(p)
            owner = index(zz, y, c)

            @pl.when(can_go(zz))
            def _():
                shard_copy(owner, send_z.at[1 + p], index(next_z(zz), y, c)).wait_send()

            shard_copy(owner, send_y.at[p], y_peer).wait_send()
            shard_copy(owner, send_c.at[p], c_peer).wait_send()

        shard_copy(index(z_at(p - 1), 1 - y, c), send_c.at[3 + p], c_peer).wait_send()
        return carry

    lax.fori_loop(1, 5, sent1, 0)

    def sent2(q, carry):
        @pl.when(z < Z - 1)
        def _():
            piece_copy(me, q, send2_z.at[q, 0], index(z + 1, y, c)).wait_send()

        @pl.when(z > 0)
        def _():
            piece_copy(me, q, send2_z.at[q, 1], index(z - 1, y, c)).wait_send()

        piece_copy(me, q, send2_y.at[q, 0], y_peer).wait_send()
        piece_copy(me, q, send2_c.at[q, 0], c_peer).wait_send()

        def body(p, inner):
            @pl.when(p <= 3)
            def _():
                zz = z_at(p)
                owner = index(zz, y, c)

                @pl.when(can_go(zz))
                def _():
                    piece_copy(
                        owner, q, send2_z.at[q, 1 + p], index(next_z(zz), y, c)
                    ).wait_send()

                piece_copy(owner, q, send2_y.at[q, p], y_peer).wait_send()
                piece_copy(owner, q, send2_c.at[q, p], c_peer).wait_send()

            piece_copy(
                index(z_at(p - 1), 1 - y, c), q, send2_c.at[q, 3 + p], c_peer
            ).wait_send()
            return inner

        return lax.fori_loop(1, 5, body, carry)

    lax.fori_loop(0, PIECES, sent2, 0)


def fused(tokens, norm_gain, w_qkv, w_out, cache_k, cache_v, lengths):
    step_count, seqs, depth = tokens.shape
    rows = step_count * seqs
    inner, out_width = w_out.shape
    head_dim = cache_k.shape[2]
    heads = inner // head_dim
    half = head_dim // 2
    freqs = jnp.exp(jnp.arange(half, dtype=jnp.float32) * (-2.0 * math.log(10000.0) / head_dim))
    positions = lengths[None, :] + jnp.arange(step_count, dtype=jnp.int32)[:, None]
    angles = positions.reshape(-1).astype(jnp.float32)[:, None] * freqs
    vmem = pl.BlockSpec(memory_space=pltpu.VMEM)
    anywhere = pl.BlockSpec(memory_space=pl.ANY)
    dma = pltpu.SemaphoreType.DMA
    result = pl.pallas_call(
        fused_kernel,
        out_shape=jax.ShapeDtypeStruct((rows, out_width), jnp.bfloat16),
        in_specs=[pl.BlockSpec(memory_space=pltpu.SMEM)] + [vmem] * 4 + [anywhere] * 4,
        out_specs=vmem,
        scratch_shapes=[
            pltpu.VMEM((WIDE, rows, depth), jnp.bfloat16),
            pltpu.VMEM((WIDE, 8, 128), jnp.float32),
            pltpu.VMEM((WIDE, depth, w_qkv.shape[1]), jnp.bfloat16),
            pltpu.VMEM((SLOTS, GROUP * head_dim, out_width), jnp.bfloat16),
            pltpu.VMEM(cache_k.shape, jnp.bfloat16),
            pltpu.VMEM(cache_v.shape, jnp.bfloat16),
            pltpu.VMEM((rows, GROUP * head_dim), jnp.float32),
            pltpu.VMEM((WIDE, 16, head_dim), jnp.bfloat16),
            pltpu.VMEM((WIDE, 16, head_dim), jnp.bfloat16),
            pltpu.VMEM((WIDE, 4 * heads, head_dim), jnp.bfloat16),
            pltpu.VMEM((rows, out_width), jnp.float32),
            pltpu.VMEM((2, rows, 128), jnp.float32),
            dma((WIDE,)),
            dma((heads // GROUP,)),
            dma((2,)),
            dma((WIDE,)),
            dma((WIDE,)),
            dma((5,)),
            dma((4,)),
            dma((8,)),
            dma((WIDE,)),
            dma((WIDE,)),
            dma((WIDE,)),
            dma((PIECES, 5)),
            dma((PIECES, 4)),
            dma((PIECES, 8)),
            dma((PIECES, WIDE)),
        ],
        compiler_params=pltpu.CompilerParams(
            collective_id=0, has_side_effects=True, vmem_limit_bytes=62 * 1024 * 1024
        ),
    )(
        lengths,
        tokens.reshape(rows, depth),
        norm_gain.reshape(WIDE, 1, depth),
        jnp.cos(angles),
        jnp.sin(angles),
        w_qkv,
        w_out,
        cache_k,
        cache_v,
    )
    return result.reshape(step_count, seqs, out_width)


def solution(mesh):
    placed = (
        P(None, "groups", "wide"),
        P(),
        P(None, "wide"),
        P(None, "wide"),
        P(("groups", "wide"), None, None),
        P(("groups", "wide"), None, None),
        P(("groups", "wide")),
    )
    return jax.shard_map(
        fused if mesh.shape["wide"] == WIDE else on_device, mesh=mesh, in_specs=placed, out_specs=P(None, "groups", "wide"), check_vma=False
    )
```

```python
import functools
import math

import jax
import jax.numpy as jnp
from jax import lax
from jax.experimental import pallas as pl
from jax.experimental.pallas import tpu as pltpu
from jax.sharding import PartitionSpec as P

norm_eps = 1e-05
MESH = pl.DeviceIdType.MESH
Z, Y, C = 4, 2, 2
WIDE = Z * Y * C
SLOTS = 8
PIECES = 4
HALVES = 2
GROUP = 4


def rotate(values, cosine, sine_table):
    half = values.shape[-1] // 2
    first = values[..., :half]
    second = values[..., half:]
    return jnp.concatenate(
        [first * cosine - second * sine_table, second * cosine + first * sine_table], axis=-1
    )


def attend(projected, cache_k, cache_v, lengths, heads, head_dim):
    step_count, seq_rows, _ = projected.shape
    width_q = heads * head_dim
    query = (
        projected[..., :width_q].astype(jnp.float32).reshape(step_count, seq_rows, heads, head_dim)
    )
    key_new = projected[..., width_q : width_q + head_dim].astype(jnp.float32)
    value_new = projected[..., width_q + head_dim :]
    positions = lengths[None, :] + jnp.arange(step_count, dtype=jnp.int32)[:, None]
    half = head_dim // 2
    freqs = jnp.exp(jnp.arange(half, dtype=jnp.float32) * (-2.0 * math.log(10000.0) / head_dim))
    angles = positions.astype(jnp.float32)[..., None] * freqs
    cosine = jnp.cos(angles)
    sine_table = jnp.sin(angles)
    query = rotate(query, cosine[:, :, None, :], sine_table[:, :, None, :]).astype(jnp.bfloat16)
    key_new = rotate(key_new, cosine, sine_table).astype(jnp.bfloat16)
    scale = 1.0 / math.sqrt(head_dim)
    cache_scores = (
        jnp.einsum("snhd,nld->snhl", query, cache_k, preferred_element_type=jnp.float32) * scale
    )
    slots = jnp.arange(cache_k.shape[1], dtype=jnp.int32)
    valid = slots[None, :] < lengths[:, None]
    cache_scores = jnp.where(valid[None, :, None, :], cache_scores, -1e30)
    new_scores = (
        jnp.einsum("snhd,tnd->snht", query, key_new, preferred_element_type=jnp.float32) * scale
    )
    order = jnp.arange(step_count, dtype=jnp.int32)
    causal = order[None, :] <= order[:, None]
    new_scores = jnp.where(causal[:, None, None, :], new_scores, -1e30)
    top = jnp.maximum(jnp.max(cache_scores, axis=-1), jnp.max(new_scores, axis=-1))
    exp_cache = jnp.exp(cache_scores - top[..., None])
    exp_new = jnp.exp(new_scores - top[..., None])
    denom = jnp.sum(exp_cache, axis=-1) + jnp.sum(exp_new, axis=-1)
    w_cache = (exp_cache / denom[..., None]).astype(jnp.bfloat16)
    w_new = (exp_new / denom[..., None]).astype(jnp.bfloat16)
    mixed = jnp.einsum("snhl,nld->snhd", w_cache, cache_v, preferred_element_type=jnp.float32)
    mixed = mixed + jnp.einsum(
        "snht,tnd->snhd", w_new, value_new, preferred_element_type=jnp.float32
    )
    return mixed.reshape(step_count, seq_rows, width_q).astype(jnp.bfloat16)


def on_device(tokens, norm_gain, w_qkv, w_out, cache_k, cache_v, lengths):
    gathered = lax.all_gather(tokens, "wide", axis=2, tiled=True)
    widened = gathered.astype(jnp.float32)
    center = jnp.mean(widened, axis=-1, keepdims=True)
    spread = jnp.mean(widened * widened, axis=-1, keepdims=True) - center * center
    normed = ((widened - center) * lax.rsqrt(spread + norm_eps) * norm_gain).astype(jnp.bfloat16)
    projected = jnp.einsum("sbd,dc->sbc", normed, w_qkv, preferred_element_type=jnp.float32)
    projected = projected.astype(jnp.bfloat16)
    per_sequence = lax.all_to_all(projected, "wide", split_axis=1, concat_axis=2, tiled=True)
    head_dim = cache_k.shape[2]
    heads = per_sequence.shape[2] // head_dim - 2
    mixed = attend(per_sequence, cache_k, cache_v, lengths, heads, head_dim)
    result = jnp.einsum(
        "snh,hd->snd",
        lax.all_gather(mixed, "wide", axis=1, tiled=True),
        w_out,
        preferred_element_type=jnp.float32,
    )
    return result.astype(jnp.bfloat16)


def iota(shape, axis):
    return lax.broadcasted_iota(jnp.int32, shape, axis)


def pick(mask):
    return jnp.where(mask, 1.0, 0.0).astype(jnp.bfloat16)


def dot(a, b):
    return jnp.dot(a, b, preferred_element_type=jnp.float32)


def dot_t(a, b):
    return lax.dot_general(a, b, (((1,), (1,)), ((), ())), preferred_element_type=jnp.float32)


def fused_kernel(
    lengths,
    tokens,
    gain,
    w_qkv,
    w_out,
    cache_k,
    cache_v,
    out,
    shards,
    stats,
    w_in,
    w_last,
    keys,
    values,
    acc,
    to_send,
    arrived,
    gathered,
    total,
    columns,
    local_sem,
    last_sem,
    cache_sem,
    stat_send,
    stat_recv,
    send1,
    recv1,
    all_send,
    all_recv,
    send2,
    recv2,
    angles,
):
    me = lax.axis_index("wide")
    z = me // (Y * C)
    y = (me // C) % Y
    c = me % C
    depth = tokens.shape[1]
    rows = tokens.shape[0]
    seqs = rows // 2
    out_depth = w_last.shape[1]
    width = w_qkv.shape[0]
    heads = w_out.shape[0] // 256
    groups = heads // GROUP
    mirrored = (z + z // 2) % 2
    upper = z // 2

    def z_at(p):
        m = p + mirrored * (1 - 2 * p) * (1 - p // 2)
        return m + upper * (3 - 2 * m)

    def index(zz, yy, cc):
        return (zz * Y + yy) * C + cc

    def remote(src, dst, send_sem, recv_sem, target):
        return pltpu.make_async_remote_copy(
            src_ref=src,
            dst_ref=dst,
            send_sem=send_sem,
            recv_sem=recv_sem,
            device_id={"wide": target},
            device_id_type=MESH,
        )

    y_peer = index(z, 1 - y, c)
    c_peer = index(z, y, 1 - c)

    def load_in(owner):
        return pltpu.make_async_copy(
            w_qkv.at[:, pl.ds(pl.multiple_of(owner * depth, depth), depth)],
            w_in.at[owner],
            local_sem.at[owner],
        )

    def load_last(g):
        return pltpu.make_async_copy(
            w_out.at[pl.ds(pl.multiple_of(g * out_depth, out_depth), out_depth)],
            w_last.at[g % SLOTS],
            last_sem.at[g],
        )

    load_keys = pltpu.make_async_copy(cache_k, keys, cache_sem.at[0])
    load_values = pltpu.make_async_copy(cache_v, values, cache_sem.at[1])

    def load_round(p, carry):
        @pl.when(p <= 3)
        def _():
            load_in(index(z_at(p), y, c)).start()
            load_in(index(z_at(p), y, 1 - c)).start()

        @pl.when(p >= 1)
        def _():
            load_in(index(z_at(p - 1), 1 - y, c)).start()
            load_in(index(z_at(p - 1), 1 - y, 1 - c)).start()

        return carry

    lax.fori_loop(0, 5, load_round, 0)

    barrier = pltpu.get_barrier_semaphore()

    def greet(k, carry):
        pl.semaphore_signal(
            barrier, inc=1, device_id={"wide": (me + k) % WIDE}, device_id_type=MESH
        )
        return carry

    lax.fori_loop(1, WIDE, greet, 0)

    widened = tokens[...].astype(jnp.float32)
    diagonal = iota((rows, 128), 0) == iota((rows, 128), 1)

    def as_row(column):
        return jnp.sum(jnp.where(diagonal, column, 0.0), axis=0, keepdims=True)

    def as_column(row):
        return jnp.sum(jnp.where(diagonal, row, 0.0), axis=1, keepdims=True)

    sums = as_row(jnp.sum(widened, axis=1, keepdims=True))
    squares = as_row(jnp.sum(widened * widened, axis=1, keepdims=True))
    line = iota((8, 128), 0)
    stats[me] = jnp.where(line == 0, sums, jnp.where(line == 1, squares, 0.0))

    pl.semaphore_wait(barrier, WIDE - 1)

    def stat_copy(k):
        return remote(
            stats.at[me], stats.at[me], stat_send.at[k], stat_recv.at[me], (me + k) % WIDE
        )

    def stat_start(k, carry):
        stat_copy(k).start()
        return carry

    lax.fori_loop(1, WIDE, stat_start, 0)

    share = rows // HALVES

    def shard_copy(owner, h, k, target):
        part = shards.at[owner, pl.ds(pl.multiple_of(h * share, share), share)]
        return remote(part, part, send1.at[h, k], recv1.at[h, owner], target)

    def own_copy(h, k, target):
        part = tokens.at[pl.ds(pl.multiple_of(h * share, share), share)]
        there = shards.at[me, pl.ds(pl.multiple_of(h * share, share), share)]
        return remote(part, there, send1.at[h, k], recv1.at[h, me], target)

    def own_start(h, carry):
        own_copy(h, 3, y_peer).start()
        own_copy(h, 7, c_peer).start()
        return carry

    lax.fori_loop(0, HALVES, own_start, 0)

    def own_z_start(j, carry):
        p = 1 + j // HALVES
        own_copy(j % HALVES, p - 1, index(z_at(p), y, c)).start()
        return carry

    lax.fori_loop(0, 3 * HALVES, own_z_start, 0)

    def arrival(owner, h):
        shard_copy(owner, h, 0, c_peer).wait_recv()

    freqs = jnp.exp(iota((8, 128), 1).astype(jnp.float32) * (-2.0 * math.log(10000.0) / 256))
    line = iota((8, 128), 0)
    position = jnp.where((line & 1) == 0, lengths[0], lengths[1]) + ((line >> 1) & 1)
    angle = position.astype(jnp.float32) * freqs
    angles[0] = jnp.cos(angle)
    angles[1] = jnp.sin(angle)
    shards[me] = tokens[...]
    acc[...] = jnp.zeros_like(acc)

    def stat_wait(k, carry):
        j = (me + k) % WIDE
        remote(stats.at[j], stats.at[j], stat_send.at[k], stat_recv.at[j], j).wait_recv()
        return carry

    lax.fori_loop(1, WIDE, stat_wait, 0)
    whole = jnp.sum(stats[...], axis=0)
    features = float(depth * WIDE)
    center = as_column(whole[0:1]) / features
    spread = as_column(whole[1:2]) / features - center * center
    columns[0] = jnp.broadcast_to(center, (rows, 128))
    columns[1] = jnp.broadcast_to(lax.rsqrt(spread + norm_eps), (rows, 128))

    def project(owner):
        load_in(owner).wait()
        x = shards[owner].astype(jnp.float32)
        normed = (x - columns[0][:, 0:1]) * columns[1][:, 0:1] * gain[owner]
        acc[:, 0:width] += dot_t(normed.astype(jnp.bfloat16), w_in[owner])

    def round1(p, carry):
        def take(h, inner):
            @pl.when(jnp.logical_and(p >= 1, p <= 3))
            def _():
                owner = index(z_at(p), y, c)
                arrival(owner, h)
                shard_copy(owner, h, 3 + p, y_peer).start()
                shard_copy(owner, h, 7 + p, c_peer).start()

            return inner

        lax.fori_loop(0, HALVES, take, 0)

        def take_y(h, inner):
            @pl.when(p >= 1)
            def _():
                owner = index(z_at(p - 1), 1 - y, c)
                arrival(owner, h)
                shard_copy(owner, h, 10 + p, c_peer).start()

            return inner

        lax.fori_loop(0, HALVES, take_y, 0)

        @pl.when(p == 2)
        def _():
            load_keys.start()
            load_values.start()

            def body(g, inner):
                load_last(g).start()
                return inner

            lax.fori_loop(0, SLOTS, body, 0)

        def part(i, inner):
            late = i // 2
            zz = z_at(p - late)

            @pl.when(jnp.logical_and(p - late >= 0, p - late <= 3))
            def _():
                owner = index(zz, (y + late) % Y, (c + i) % C)

                @pl.when(i % 2 == 1)
                def _():
                    def body(h, deep):
                        arrival(owner, h)
                        return deep

                    lax.fori_loop(0, HALVES, body, 0)

                project(owner)

            return inner

        return lax.fori_loop(0, 4, part, carry)

    lax.fori_loop(0, 5, round1, 0)

    offset = (width * me) % 256
    shifted = pltpu.roll(acc[...], offset, 1).astype(jnp.bfloat16)
    row = iota((WIDE * 16, rows), 0)
    token = ((row >> 1) & 1) * seqs + 2 * (row >> 4) + (row & 1)
    chosen = iota((WIDE * 16, rows), 1) == token
    sending = jnp.zeros((WIDE * 16, 256), jnp.float32)
    for hh in range(GROUP):
        sending += dot(
            pick(jnp.logical_and(chosen, ((row >> 2) & 3) == hh)),
            shifted[:, hh * 256 : (hh + 1) * 256],
        )
    to_send[...] = sending.astype(jnp.bfloat16).reshape(to_send.shape)

    def all_copy(k):
        t = (me + k) % WIDE
        return remote(to_send.at[t], arrived.at[me], all_send.at[k], all_recv.at[me], t)

    def all_start(k, carry):
        all_copy(k).start()
        return carry

    lax.fori_loop(1, WIDE, all_start, 0)
    arrived[me] = to_send[me]
    load_keys.wait()
    load_values.wait()

    def all_wait(k, carry):
        j = (me + k) % WIDE
        remote(to_send.at[j], arrived.at[j], all_send.at[k], all_recv.at[j], j).wait_recv()
        return carry

    lax.fori_loop(1, WIDE, all_wait, 0)

    blocks = arrived[...].reshape(WIDE * 16, 256)
    query_rows = 2 * heads
    col = iota((query_rows + 16, WIDE * 16), 1)
    head = ((width * (col >> 4)) >> 8) + ((col >> 2) & 3)
    step = (col >> 1) & 1
    target = jnp.where(
        head < heads, step * heads + head, query_rows + 8 * (head - heads) + step
    )
    placed = iota((query_rows + 16, WIDE * 16), 0) == target
    scale = 1.0 / math.sqrt(256)
    slots = keys.shape[1]
    sending = jnp.zeros((4 * heads, 256), jnp.float32)
    for n in range(2):
        mine = dot(pick(jnp.logical_and(placed, (col & 1) == n)), blocks)

        def turn(block, cosine, sine_table):
            first, second = block[:, 0:128], block[:, 128:256]
            return jnp.concatenate(
                [first * cosine - second * sine_table, second * cosine + first * sine_table],
                axis=1,
            ).astype(jnp.bfloat16)

        def by_step(table, count, half):
            at = iota((count, 128), 0)
            return jnp.where(at < half, table[n : n + 1, :], table[n + 2 : n + 3, :])

        query = turn(
            mine[0:query_rows],
            by_step(angles[0], query_rows, heads),
            by_step(angles[1], query_rows, heads),
        )
        key_new = turn(
            mine[query_rows : query_rows + 8], by_step(angles[0], 8, 1), by_step(angles[1], 8, 1)
        )
        value_new = mine[query_rows + 8 : query_rows + 16].astype(jnp.bfloat16)
        scores = dot_t(query, keys[n]) * scale
        scores = jnp.where(iota((query_rows, slots), 1) < lengths[n], scores, -1e30)
        fresh = dot_t(query, key_new) * scale
        t = iota((query_rows, 8), 1)
        s = jnp.where(iota((query_rows, 8), 0) >= heads, 1, 0)
        fresh = jnp.where(t <= s, fresh, -1e30)
        top = jnp.maximum(
            jnp.max(scores, axis=1, keepdims=True), jnp.max(fresh, axis=1, keepdims=True)
        )
        scores = jnp.exp(scores - top)
        fresh = jnp.exp(fresh - top)
        denom = jnp.sum(scores, axis=1, keepdims=True) + jnp.sum(fresh, axis=1, keepdims=True)
        inverse = 1.0 / denom
        mixed = dot((scores * inverse).astype(jnp.bfloat16), values[n])
        mixed += dot((fresh * inverse).astype(jnp.bfloat16), value_new)
        at = iota((4 * heads, query_rows), 0)
        from_row = ((at >> 1) & 1) * heads + (at >> 2)
        sending += dot(
            pick(
                jnp.logical_and(
                    iota((4 * heads, query_rows), 1) == from_row, (at & 1) == n
                )
            ),
            mixed.astype(jnp.bfloat16),
        )
    gathered[me] = sending.astype(jnp.bfloat16)

    high = gathered.shape[1] // PIECES

    def piece_copy(owner, q, k, target):
        part = gathered.at[owner, pl.ds(pl.multiple_of(q * high, high), high)]
        return remote(part, part, send2.at[q, k], recv2.at[q, owner], target)

    def piece_start(q, carry):
        piece_copy(me, q, 3, y_peer).start()
        piece_copy(me, q, 7, c_peer).start()

        def body(p, inner):
            piece_copy(me, q, p - 1, index(z_at(p), y, c)).start()
            return inner

        return lax.fori_loop(1, 4, body, carry)

    lax.fori_loop(0, PIECES, piece_start, 0)

    def piece_arrival(owner, q):
        piece_copy(owner, q, 0, c_peer).wait_recv()

    def forward(q, p):
        owner = index(z_at(p), y, c)
        piece_arrival(owner, q)
        piece_copy(owner, q, 3 + p, y_peer).start()
        piece_copy(owner, q, 7 + p, c_peer).start()

    def forward_y(q, p):
        owner = index(z_at(p), 1 - y, c)
        piece_arrival(owner, q)
        piece_copy(owner, q, 11 + p, c_peer).start()

    def stage_a(q):
        def body(p, inner):
            forward(q, p)
            return inner

        lax.fori_loop(1, 4, body, 0)

    def stage_b(q):
        def body(p, inner):
            forward_y(q, p)
            return inner

        lax.fori_loop(0, 4, body, 0)

    def stage_c(q):
        def body(j, inner):
            piece_arrival(index(z_at(j // 2), (y + j) % Y, 1 - c), q)
            return inner

        lax.fori_loop(0, 8, body, 0)

    total[...] = jnp.zeros_like(total)
    per_piece = groups // PIECES
    i = iota((rows * GROUP, WIDE * 16), 0)
    m = i % rows
    b = m % seqs
    source = (b >> 1) * 16 + (i // rows) * 4 + (m // seqs) * 2 + (b & 1)
    reorder = pick(iota((rows * GROUP, WIDE * 16), 1) == source)

    def multiply(g, carry):
        @pl.when(g % per_piece == 0)
        def _():
            q = g // per_piece

            @pl.when(q < PIECES - 2)
            def _():
                stage_a(q + 2)

            @pl.when(q < PIECES - 1)
            def _():
                stage_b(q + 1)

            stage_c(q)

        load_last(g).wait()
        block = gathered[:, pl.ds(pl.multiple_of(g * 16, 16), 16), :].reshape(WIDE * 16, 256)
        ordered = dot(reorder, block).astype(jnp.bfloat16)
        lined = jnp.concatenate(
            [ordered[h * rows : (h + 1) * rows] for h in range(GROUP)], axis=1
        )
        total[...] += dot(lined, w_last[g % SLOTS])

        @pl.when(g + SLOTS < groups)
        def _():
            load_last(g + SLOTS).start()

        return carry

    stage_a(0)
    stage_a(1)
    stage_b(0)
    lax.fori_loop(0, groups, multiply, 0)
    out[...] = total[...].astype(jnp.bfloat16)

    def sent(k, carry):
        stat_copy(k).wait_send()
        all_copy(k).wait_send()
        return carry

    lax.fori_loop(1, WIDE, sent, 0)

    def sent1(k, carry):
        def body(h, inner):
            own_copy(h, k, c_peer).wait_send()
            return inner

        return lax.fori_loop(0, HALVES, body, carry)

    lax.fori_loop(0, 15, sent1, 0)

    def sent2(k, carry):
        def body(q, inner):
            piece_copy(me, q, k, c_peer).wait_send()
            return inner

        return lax.fori_loop(0, PIECES, body, carry)

    lax.fori_loop(0, 15, sent2, 0)


def fused(tokens, norm_gain, w_qkv, w_out, cache_k, cache_v, lengths):
    step_count, seqs, depth = tokens.shape
    rows = step_count * seqs
    inner, out_width = w_out.shape
    head_dim = cache_k.shape[2]
    heads = inner // head_dim
    vmem = pl.BlockSpec(memory_space=pltpu.VMEM)
    anywhere = pl.BlockSpec(memory_space=pl.ANY)
    dma = pltpu.SemaphoreType.DMA
    result = pl.pallas_call(
        fused_kernel,
        out_shape=jax.ShapeDtypeStruct((rows, out_width), jnp.bfloat16),
        in_specs=[pl.BlockSpec(memory_space=pltpu.SMEM)] + [vmem] * 2 + [anywhere] * 4,
        out_specs=vmem,
        scratch_shapes=[
            pltpu.VMEM((WIDE, rows, depth), jnp.bfloat16),
            pltpu.VMEM((WIDE, 8, 128), jnp.float32),
            pltpu.VMEM((WIDE, w_qkv.shape[1], depth), jnp.bfloat16),
            pltpu.VMEM((SLOTS, GROUP * head_dim, out_width), jnp.bfloat16),
            pltpu.VMEM(cache_k.shape, jnp.bfloat16),
            pltpu.VMEM(cache_v.shape, jnp.bfloat16),
            pltpu.VMEM((rows, GROUP * head_dim), jnp.float32),
            pltpu.VMEM((WIDE, 16, head_dim), jnp.bfloat16),
            pltpu.VMEM((WIDE, 16, head_dim), jnp.bfloat16),
            pltpu.VMEM((WIDE, 4 * heads, head_dim), jnp.bfloat16),
            pltpu.VMEM((rows, out_width), jnp.float32),
            pltpu.VMEM((2, rows, 128), jnp.float32),
            dma((WIDE,)),
            dma((heads // GROUP,)),
            dma((2,)),
            dma((WIDE,)),
            dma((WIDE,)),
            dma((HALVES, 15)),
            dma((HALVES, WIDE)),
            dma((WIDE,)),
            dma((WIDE,)),
            dma((PIECES, 15)),
            dma((PIECES, WIDE)),
            pltpu.VMEM((2, 8, 128), jnp.float32),
        ],
        compiler_params=pltpu.CompilerParams(
            collective_id=0, has_side_effects=True, vmem_limit_bytes=62 * 1024 * 1024
        ),
    )(
        lengths,
        tokens.reshape(rows, depth),
        norm_gain.reshape(WIDE, 1, depth),
        w_qkv.T,
        w_out,
        cache_k,
        cache_v,
    )
    return result.reshape(step_count, seqs, out_width)


def solution(mesh):
    placed = (
        P(None, "groups", "wide"),
        P(),
        P(None, "wide"),
        P(None, "wide"),
        P(("groups", "wide"), None, None),
        P(("groups", "wide"), None, None),
        P(("groups", "wide")),
    )
    return jax.shard_map(
        fused if mesh.shape["wide"] == WIDE else on_device, mesh=mesh, in_specs=placed, out_specs=P(None, "groups", "wide"), check_vma=False
    )
```

```python
import functools
import math

import jax
import jax.numpy as jnp
from jax import lax
from jax.experimental import pallas as pl
from jax.experimental.pallas import tpu as pltpu
from jax.sharding import PartitionSpec as P

norm_eps = 1e-05
MESH = pl.DeviceIdType.MESH
Z, Y, C = 4, 2, 2
WIDE = Z * Y * C
SLOTS = 8
PIECES = 4
HALVES = 4
GROUP = 4


def rotate(values, cosine, sine_table):
    half = values.shape[-1] // 2
    first = values[..., :half]
    second = values[..., half:]
    return jnp.concatenate(
        [first * cosine - second * sine_table, second * cosine + first * sine_table], axis=-1
    )


def attend(projected, cache_k, cache_v, lengths, heads, head_dim):
    step_count, seq_rows, _ = projected.shape
    width_q = heads * head_dim
    query = (
        projected[..., :width_q].astype(jnp.float32).reshape(step_count, seq_rows, heads, head_dim)
    )
    key_new = projected[..., width_q : width_q + head_dim].astype(jnp.float32)
    value_new = projected[..., width_q + head_dim :]
    positions = lengths[None, :] + jnp.arange(step_count, dtype=jnp.int32)[:, None]
    half = head_dim // 2
    freqs = jnp.exp(jnp.arange(half, dtype=jnp.float32) * (-2.0 * math.log(10000.0) / head_dim))
    angles = positions.astype(jnp.float32)[..., None] * freqs
    cosine = jnp.cos(angles)
    sine_table = jnp.sin(angles)
    query = rotate(query, cosine[:, :, None, :], sine_table[:, :, None, :]).astype(jnp.bfloat16)
    key_new = rotate(key_new, cosine, sine_table).astype(jnp.bfloat16)
    scale = 1.0 / math.sqrt(head_dim)
    cache_scores = (
        jnp.einsum("snhd,nld->snhl", query, cache_k, preferred_element_type=jnp.float32) * scale
    )
    slots = jnp.arange(cache_k.shape[1], dtype=jnp.int32)
    valid = slots[None, :] < lengths[:, None]
    cache_scores = jnp.where(valid[None, :, None, :], cache_scores, -1e30)
    new_scores = (
        jnp.einsum("snhd,tnd->snht", query, key_new, preferred_element_type=jnp.float32) * scale
    )
    order = jnp.arange(step_count, dtype=jnp.int32)
    causal = order[None, :] <= order[:, None]
    new_scores = jnp.where(causal[:, None, None, :], new_scores, -1e30)
    top = jnp.maximum(jnp.max(cache_scores, axis=-1), jnp.max(new_scores, axis=-1))
    exp_cache = jnp.exp(cache_scores - top[..., None])
    exp_new = jnp.exp(new_scores - top[..., None])
    denom = jnp.sum(exp_cache, axis=-1) + jnp.sum(exp_new, axis=-1)
    w_cache = (exp_cache / denom[..., None]).astype(jnp.bfloat16)
    w_new = (exp_new / denom[..., None]).astype(jnp.bfloat16)
    mixed = jnp.einsum("snhl,nld->snhd", w_cache, cache_v, preferred_element_type=jnp.float32)
    mixed = mixed + jnp.einsum(
        "snht,tnd->snhd", w_new, value_new, preferred_element_type=jnp.float32
    )
    return mixed.reshape(step_count, seq_rows, width_q).astype(jnp.bfloat16)


def on_device(tokens, norm_gain, w_qkv, w_out, cache_k, cache_v, lengths):
    gathered = lax.all_gather(tokens, "wide", axis=2, tiled=True)
    widened = gathered.astype(jnp.float32)
    center = jnp.mean(widened, axis=-1, keepdims=True)
    spread = jnp.mean(widened * widened, axis=-1, keepdims=True) - center * center
    normed = ((widened - center) * lax.rsqrt(spread + norm_eps) * norm_gain).astype(jnp.bfloat16)
    projected = jnp.einsum("sbd,dc->sbc", normed, w_qkv, preferred_element_type=jnp.float32)
    projected = projected.astype(jnp.bfloat16)
    per_sequence = lax.all_to_all(projected, "wide", split_axis=1, concat_axis=2, tiled=True)
    head_dim = cache_k.shape[2]
    heads = per_sequence.shape[2] // head_dim - 2
    mixed = attend(per_sequence, cache_k, cache_v, lengths, heads, head_dim)
    result = jnp.einsum(
        "snh,hd->snd",
        lax.all_gather(mixed, "wide", axis=1, tiled=True),
        w_out,
        preferred_element_type=jnp.float32,
    )
    return result.astype(jnp.bfloat16)


def iota(shape, axis):
    return lax.broadcasted_iota(jnp.int32, shape, axis)


def pick(mask):
    return jnp.where(mask, 1.0, 0.0).astype(jnp.bfloat16)


def dot(a, b):
    return jnp.dot(a, b, preferred_element_type=jnp.float32)


def dot_t(a, b):
    return lax.dot_general(a, b, (((1,), (1,)), ((), ())), preferred_element_type=jnp.float32)


def fused_kernel(
    lengths,
    tokens,
    gain,
    w_qkv,
    w_out,
    cache_k,
    cache_v,
    out,
    shards,
    stats,
    w_in,
    w_last,
    keys,
    values,
    acc,
    to_send,
    arrived,
    gathered,
    total,
    columns,
    local_sem,
    last_sem,
    cache_sem,
    stat_send,
    stat_recv,
    send1,
    recv1,
    near1,
    all_send,
    all_recv,
    send2,
    recv2,
    near2,
    angles,
):
    me = lax.axis_index("wide")
    z = me // (Y * C)
    y = (me // C) % Y
    c = me % C
    depth = tokens.shape[1]
    rows = tokens.shape[0]
    seqs = rows // 2
    out_depth = w_last.shape[1]
    width = w_qkv.shape[0]
    heads = w_out.shape[0] // 256
    groups = heads // GROUP
    mirrored = (z + z // 2) % 2
    upper = z // 2

    def z_at(p):
        m = p + mirrored * (1 - 2 * p) * (1 - p // 2)
        return m + upper * (3 - 2 * m)

    def index(zz, yy, cc):
        return (zz * Y + yy) * C + cc

    def remote(src, dst, send_sem, recv_sem, target):
        return pltpu.make_async_remote_copy(
            src_ref=src,
            dst_ref=dst,
            send_sem=send_sem,
            recv_sem=recv_sem,
            device_id={"wide": target},
            device_id_type=MESH,
        )

    y_peer = index(z, 1 - y, c)
    c_peer = index(z, y, 1 - c)

    def next_z(zz):
        return z + jnp.where(zz > z, -1, 1)

    def can_go(zz):
        after = next_z(zz)
        return jnp.logical_and(after >= 0, after < Z)

    def send_own(copy, h):
        @pl.when(z < Z - 1)
        def _():
            copy(me, h, 0, index(z + 1, y, c)).start()

        @pl.when(z > 0)
        def _():
            copy(me, h, 0, index(z - 1, y, c)).start()

        copy(me, h, 1, y_peer).start()
        copy(me, h, 2, c_peer).start()

    def pass_on(copy, h, p):
        zz = z_at(p)
        owner = index(zz, y, c)
        copy(owner, h, 0, c_peer).wait_recv()

        @pl.when(can_go(zz))
        def _():
            copy(owner, h, 0, index(next_z(zz), y, c)).start()

        copy(owner, h, 1, y_peer).start()
        copy(owner, h, 2, c_peer).start()

    def pass_y(copy, h, p):
        owner = index(z_at(p), 1 - y, c)
        copy(owner, h, 1, c_peer).wait_recv()
        copy(owner, h, 2, c_peer).start()

    def all_sent(buffer, sems):
        def sent(count, kind):
            part = buffer.at[pl.ds(0, count)]
            remote(part, part, sems.at[kind], sems.at[kind], c_peer).wait_send()

        @pl.when(mirrored == 1)
        def _():
            sent(5, 0)

        @pl.when(mirrored == 0)
        def _():
            sent(1, 0)

        sent(4, 1)
        sent(8, 2)

    def load_in(owner):
        return pltpu.make_async_copy(
            w_qkv.at[:, pl.ds(pl.multiple_of(owner * depth, depth), depth)],
            w_in.at[owner],
            local_sem.at[owner],
        )

    def load_last(g):
        return pltpu.make_async_copy(
            w_out.at[pl.ds(pl.multiple_of(g * out_depth, out_depth), out_depth)],
            w_last.at[g % SLOTS],
            last_sem.at[g],
        )

    load_keys = pltpu.make_async_copy(cache_k, keys, cache_sem.at[0])
    load_values = pltpu.make_async_copy(cache_v, values, cache_sem.at[1])

    def load_round(p, carry):
        @pl.when(p <= 3)
        def _():
            load_in(index(z_at(p), y, c)).start()
            load_in(index(z_at(p), y, 1 - c)).start()

        @pl.when(p >= 1)
        def _():
            load_in(index(z_at(p - 1), 1 - y, c)).start()
            load_in(index(z_at(p - 1), 1 - y, 1 - c)).start()

        return carry

    lax.fori_loop(0, 5, load_round, 0)

    barrier = pltpu.get_barrier_semaphore()

    def greet(k, carry):
        pl.semaphore_signal(
            barrier, inc=1, device_id={"wide": (me + k) % WIDE}, device_id_type=MESH
        )
        return carry

    lax.fori_loop(1, WIDE, greet, 0)

    widened = tokens[...].astype(jnp.float32)
    diagonal = iota((rows, 128), 0) == iota((rows, 128), 1)

    def as_row(column):
        return jnp.sum(jnp.where(diagonal, column, 0.0), axis=0, keepdims=True)

    def as_column(row):
        return jnp.sum(jnp.where(diagonal, row, 0.0), axis=1, keepdims=True)

    sums = as_row(jnp.sum(widened, axis=1, keepdims=True))
    squares = as_row(jnp.sum(widened * widened, axis=1, keepdims=True))
    line = iota((8, 128), 0)
    stats[me] = jnp.where(line == 0, sums, jnp.where(line == 1, squares, 0.0))

    pl.semaphore_wait(barrier, WIDE - 1)

    def stat_copy(k):
        return remote(
            stats.at[me], stats.at[me], stat_send.at[0], stat_recv.at[0], (me + k) % WIDE
        )

    def stat_start(k, carry):
        stat_copy(k).start()
        return carry

    lax.fori_loop(1, WIDE, stat_start, 0)

    share = rows // HALVES

    def into(owner, h, k):
        return near1.at[owner] if k == 2 else recv1.at[h, owner]

    def shard_copy(owner, h, k, target):
        part = shards.at[owner, pl.ds(pl.multiple_of(h * share, share), share)]
        return remote(part, part, send1.at[k], into(owner, h, k), target)

    def own_copy(owner, h, k, target):
        part = tokens.at[pl.ds(pl.multiple_of(h * share, share), share)]
        there = shards.at[me, pl.ds(pl.multiple_of(h * share, share), share)]
        return remote(part, there, send1.at[k], into(me, h, k), target)

    def own_start(h, carry):
        send_own(own_copy, h)
        return carry

    lax.fori_loop(0, HALVES, own_start, 0)

    freqs = jnp.exp(iota((8, 128), 1).astype(jnp.float32) * (-2.0 * math.log(10000.0) / 256))
    line = iota((8, 128), 0)
    position = jnp.where((line & 1) == 0, lengths[0], lengths[1]) + ((line >> 1) & 1)
    angle = position.astype(jnp.float32) * freqs
    angles[0] = jnp.cos(angle)
    angles[1] = jnp.sin(angle)
    shards[me] = tokens[...]
    acc[...] = jnp.zeros_like(acc)

    others = stats.at[pl.ds(0, WIDE - 1)]
    remote(others, others, stat_send.at[0], stat_recv.at[0], c_peer).wait_recv()
    whole = jnp.sum(stats[...], axis=0)
    features = float(depth * WIDE)
    center = as_column(whole[0:1]) / features
    spread = as_column(whole[1:2]) / features - center * center
    columns[0] = jnp.broadcast_to(center, (rows, 128))
    columns[1] = jnp.broadcast_to(lax.rsqrt(spread + norm_eps), (rows, 128))

    def project(owner):
        load_in(owner).wait()
        x = shards[owner].astype(jnp.float32)
        normed = (x - columns[0][:, 0:1]) * columns[1][:, 0:1] * gain[owner]
        acc[:, 0:width] += dot_t(normed.astype(jnp.bfloat16), w_in[owner])

    def round1(p, carry):
        @pl.when(p == 2)
        def _():
            load_keys.start()
            load_values.start()

            def body(g, inner):
                load_last(g).start()
                return inner

            lax.fori_loop(0, SLOTS, body, 0)

        def part(i, inner):
            @pl.when(jnp.logical_and(p >= 1, p <= 3))
            def _():
                pass_on(shard_copy, i, p)

            @pl.when(jnp.logical_and(p >= 1, p <= 4))
            def _():
                pass_y(shard_copy, i, p - 1)

            late = 1 + i // 2

            @pl.when(jnp.logical_and(p - late >= 0, p - late <= 3))
            def _():
                owner = index(z_at(p - late), (y + i // 2) % Y, (c + i) % C)

                @pl.when(i % 2 == 1)
                def _():
                    whole_shard = shards.at[owner]
                    remote(
                        whole_shard, whole_shard, send1.at[2], near1.at[owner], c_peer
                    ).wait_recv()

                project(owner)

            return inner

        return lax.fori_loop(0, HALVES, part, carry)

    lax.fori_loop(0, 6, round1, 0)

    offset = (width * me) % 256
    shifted = pltpu.roll(acc[...], offset, 1).astype(jnp.bfloat16)
    row = iota((WIDE * 16, rows), 0)
    token = ((row >> 1) & 1) * seqs + 2 * (row >> 4) + (row & 1)
    chosen = iota((WIDE * 16, rows), 1) == token
    sending = jnp.zeros((WIDE * 16, 256), jnp.float32)
    for hh in range(GROUP):
        sending += dot(
            pick(jnp.logical_and(chosen, ((row >> 2) & 3) == hh)),
            shifted[:, hh * 256 : (hh + 1) * 256],
        )
    to_send[...] = sending.astype(jnp.bfloat16).reshape(to_send.shape)

    def all_copy(k):
        t = (me + k) % WIDE
        return remote(to_send.at[t], arrived.at[me], all_send.at[0], all_recv.at[0], t)

    def all_start(k, carry):
        all_copy(k).start()
        return carry

    lax.fori_loop(1, WIDE, all_start, 0)
    arrived[me] = to_send[me]
    load_keys.wait()
    load_values.wait()

    received = arrived.at[pl.ds(0, WIDE - 1)]
    remote(received, received, all_send.at[0], all_recv.at[0], c_peer).wait_recv()

    blocks = arrived[...].reshape(WIDE * 16, 256)
    query_rows = 2 * heads
    col = iota((query_rows + 16, WIDE * 16), 1)
    head = ((width * (col >> 4)) >> 8) + ((col >> 2) & 3)
    step = (col >> 1) & 1
    target = jnp.where(
        head < heads, step * heads + head, query_rows + 8 * (head - heads) + step
    )
    placed = iota((query_rows + 16, WIDE * 16), 0) == target
    scale = 1.0 / math.sqrt(256)
    slots = keys.shape[1]
    sending = jnp.zeros((4 * heads, 256), jnp.float32)
    for n in range(2):
        mine = dot(pick(jnp.logical_and(placed, (col & 1) == n)), blocks)

        def turn(block, cosine, sine_table):
            first, second = block[:, 0:128], block[:, 128:256]
            return jnp.concatenate(
                [first * cosine - second * sine_table, second * cosine + first * sine_table],
                axis=1,
            ).astype(jnp.bfloat16)

        def by_step(table, count, half):
            at = iota((count, 128), 0)
            return jnp.where(at < half, table[n : n + 1, :], table[n + 2 : n + 3, :])

        query = turn(
            mine[0:query_rows],
            by_step(angles[0], query_rows, heads),
            by_step(angles[1], query_rows, heads),
        )
        key_new = turn(
            mine[query_rows : query_rows + 8], by_step(angles[0], 8, 1), by_step(angles[1], 8, 1)
        )
        value_new = mine[query_rows + 8 : query_rows + 16].astype(jnp.bfloat16)
        scores = dot_t(query, keys[n]) * scale
        scores = jnp.where(iota((query_rows, slots), 1) < lengths[n], scores, -1e30)
        fresh = dot_t(query, key_new) * scale
        t = iota((query_rows, 8), 1)
        s = jnp.where(iota((query_rows, 8), 0) >= heads, 1, 0)
        fresh = jnp.where(t <= s, fresh, -1e30)
        top = jnp.maximum(
            jnp.max(scores, axis=1, keepdims=True), jnp.max(fresh, axis=1, keepdims=True)
        )
        scores = jnp.exp(scores - top)
        fresh = jnp.exp(fresh - top)
        denom = jnp.sum(scores, axis=1, keepdims=True) + jnp.sum(fresh, axis=1, keepdims=True)
        inverse = 1.0 / denom
        mixed = dot((scores * inverse).astype(jnp.bfloat16), values[n])
        mixed += dot((fresh * inverse).astype(jnp.bfloat16), value_new)
        at = iota((4 * heads, query_rows), 0)
        from_row = ((at >> 1) & 1) * heads + (at >> 2)
        sending += dot(
            pick(
                jnp.logical_and(
                    iota((4 * heads, query_rows), 1) == from_row, (at & 1) == n
                )
            ),
            mixed.astype(jnp.bfloat16),
        )
    gathered[me] = sending.astype(jnp.bfloat16)

    high = gathered.shape[1] // PIECES

    def piece_copy(owner, q, k, target):
        part = gathered.at[owner, pl.ds(pl.multiple_of(q * high, high), high)]
        arrives = near2.at[q] if k == 2 else recv2.at[q, owner]
        return remote(part, part, send2.at[k], arrives, target)

    def piece_start(q, carry):
        send_own(piece_copy, q)
        return carry

    lax.fori_loop(0, PIECES, piece_start, 0)

    def pass_round(p, carry):
        def body(q, inner):
            pass_on(piece_copy, q, p)
            pass_y(piece_copy, q, p - 1)
            return inner

        return lax.fori_loop(0, PIECES, body, carry)

    lax.fori_loop(1, Z, pass_round, 0)

    def stage_c(q):
        part = gathered.at[pl.ds(0, WIDE // 2), pl.ds(0, high)]
        remote(part, part, send2.at[2], near2.at[q], c_peer).wait_recv()

    total[...] = jnp.zeros_like(total)
    per_piece = groups // PIECES
    i = iota((rows * GROUP, WIDE * 16), 0)
    m = i % rows
    b = m % seqs
    source = (b >> 1) * 16 + (i // rows) * 4 + (m // seqs) * 2 + (b & 1)
    reorder = pick(iota((rows * GROUP, WIDE * 16), 1) == source)

    def multiply(g, carry):
        @pl.when(g % per_piece == 0)
        def _():
            q = g // per_piece

            @pl.when(q < PIECES - 1)
            def _():
                pass_y(piece_copy, q + 1, 3)

            stage_c(q)

        load_last(g).wait()
        block = gathered[:, pl.ds(pl.multiple_of(g * 16, 16), 16), :].reshape(WIDE * 16, 256)
        ordered = dot(reorder, block).astype(jnp.bfloat16)
        lined = jnp.concatenate(
            [ordered[h * rows : (h + 1) * rows] for h in range(GROUP)], axis=1
        )
        total[...] += dot(lined, w_last[g % SLOTS])

        @pl.when(g + SLOTS < groups)
        def _():
            load_last(g + SLOTS).start()

        return carry

    pass_y(piece_copy, 0, 3)
    lax.fori_loop(0, groups, multiply, 0)
    out[...] = total[...].astype(jnp.bfloat16)

    remote(others, others, stat_send.at[0], stat_recv.at[0], c_peer).wait_send()
    left = to_send.at[pl.ds(0, WIDE - 1)]
    remote(left, left, all_send.at[0], all_recv.at[0], c_peer).wait_send()
    all_sent(shards, send1)
    all_sent(gathered, send2)


def fused(tokens, norm_gain, w_qkv, w_out, cache_k, cache_v, lengths):
    step_count, seqs, depth = tokens.shape
    rows = step_count * seqs
    inner, out_width = w_out.shape
    head_dim = cache_k.shape[2]
    heads = inner // head_dim
    vmem = pl.BlockSpec(memory_space=pltpu.VMEM)
    anywhere = pl.BlockSpec(memory_space=pl.ANY)
    dma = pltpu.SemaphoreType.DMA
    result = pl.pallas_call(
        fused_kernel,
        out_shape=jax.ShapeDtypeStruct((rows, out_width), jnp.bfloat16),
        in_specs=[pl.BlockSpec(memory_space=pltpu.SMEM)] + [vmem] * 2 + [anywhere] * 4,
        out_specs=vmem,
        scratch_shapes=[
            pltpu.VMEM((WIDE, rows, depth), jnp.bfloat16),
            pltpu.VMEM((WIDE, 8, 128), jnp.float32),
            pltpu.VMEM((WIDE, w_qkv.shape[1], depth), jnp.bfloat16),
            pltpu.VMEM((SLOTS, GROUP * head_dim, out_width), jnp.bfloat16),
            pltpu.VMEM(cache_k.shape, jnp.bfloat16),
            pltpu.VMEM(cache_v.shape, jnp.bfloat16),
            pltpu.VMEM((rows, GROUP * head_dim), jnp.float32),
            pltpu.VMEM((WIDE, 16, head_dim), jnp.bfloat16),
            pltpu.VMEM((WIDE, 16, head_dim), jnp.bfloat16),
            pltpu.VMEM((WIDE, 4 * heads, head_dim), jnp.bfloat16),
            pltpu.VMEM((rows, out_width), jnp.float32),
            pltpu.VMEM((2, rows, 128), jnp.float32),
            dma((WIDE,)),
            dma((heads // GROUP,)),
            dma((2,)),
            dma((1,)),
            dma((1,)),
            dma((3,)),
            dma((HALVES, WIDE)),
            dma((WIDE,)),
            dma((1,)),
            dma((1,)),
            dma((3,)),
            dma((PIECES, WIDE)),
            dma((PIECES,)),
            pltpu.VMEM((2, 8, 128), jnp.float32),
        ],
        compiler_params=pltpu.CompilerParams(
            collective_id=0, has_side_effects=True, vmem_limit_bytes=62 * 1024 * 1024
        ),
    )(
        lengths,
        tokens.reshape(rows, depth),
        norm_gain.reshape(WIDE, 1, depth),
        w_qkv.T,
        w_out,
        cache_k,
        cache_v,
    )
    return result.reshape(step_count, seqs, out_width)


def solution(mesh):
    placed = (
        P(None, "groups", "wide"),
        P(),
        P(None, "wide"),
        P(None, "wide"),
        P(("groups", "wide"), None, None),
        P(("groups", "wide"), None, None),
        P(("groups", "wide")),
    )
    return jax.shard_map(
        fused if mesh.shape["wide"] == WIDE else on_device, mesh=mesh, in_specs=placed, out_specs=P(None, "groups", "wide"), check_vma=False
    )
```

```python
import functools
import math

import jax
import jax.numpy as jnp
from jax import lax
from jax.experimental import pallas as pl
from jax.experimental.pallas import tpu as pltpu
from jax.sharding import PartitionSpec as P

norm_eps = 1e-05
MESH = pl.DeviceIdType.MESH
Z, Y, C = 4, 2, 2
WIDE = Z * Y * C
SLOTS = 8
PIECES = 4
HALVES = 4
GROUP = 4


def rotate(values, cosine, sine_table):
    half = values.shape[-1] // 2
    first = values[..., :half]
    second = values[..., half:]
    return jnp.concatenate(
        [first * cosine - second * sine_table, second * cosine + first * sine_table], axis=-1
    )


def attend(projected, cache_k, cache_v, lengths, heads, head_dim):
    step_count, seq_rows, _ = projected.shape
    width_q = heads * head_dim
    query = (
        projected[..., :width_q].astype(jnp.float32).reshape(step_count, seq_rows, heads, head_dim)
    )
    key_new = projected[..., width_q : width_q + head_dim].astype(jnp.float32)
    value_new = projected[..., width_q + head_dim :]
    positions = lengths[None, :] + jnp.arange(step_count, dtype=jnp.int32)[:, None]
    half = head_dim // 2
    freqs = jnp.exp(jnp.arange(half, dtype=jnp.float32) * (-2.0 * math.log(10000.0) / head_dim))
    angles = positions.astype(jnp.float32)[..., None] * freqs
    cosine = jnp.cos(angles)
    sine_table = jnp.sin(angles)
    query = rotate(query, cosine[:, :, None, :], sine_table[:, :, None, :]).astype(jnp.bfloat16)
    key_new = rotate(key_new, cosine, sine_table).astype(jnp.bfloat16)
    scale = 1.0 / math.sqrt(head_dim)
    cache_scores = (
        jnp.einsum("snhd,nld->snhl", query, cache_k, preferred_element_type=jnp.float32) * scale
    )
    slots = jnp.arange(cache_k.shape[1], dtype=jnp.int32)
    valid = slots[None, :] < lengths[:, None]
    cache_scores = jnp.where(valid[None, :, None, :], cache_scores, -1e30)
    new_scores = (
        jnp.einsum("snhd,tnd->snht", query, key_new, preferred_element_type=jnp.float32) * scale
    )
    order = jnp.arange(step_count, dtype=jnp.int32)
    causal = order[None, :] <= order[:, None]
    new_scores = jnp.where(causal[:, None, None, :], new_scores, -1e30)
    top = jnp.maximum(jnp.max(cache_scores, axis=-1), jnp.max(new_scores, axis=-1))
    exp_cache = jnp.exp(cache_scores - top[..., None])
    exp_new = jnp.exp(new_scores - top[..., None])
    denom = jnp.sum(exp_cache, axis=-1) + jnp.sum(exp_new, axis=-1)
    w_cache = (exp_cache / denom[..., None]).astype(jnp.bfloat16)
    w_new = (exp_new / denom[..., None]).astype(jnp.bfloat16)
    mixed = jnp.einsum("snhl,nld->snhd", w_cache, cache_v, preferred_element_type=jnp.float32)
    mixed = mixed + jnp.einsum(
        "snht,tnd->snhd", w_new, value_new, preferred_element_type=jnp.float32
    )
    return mixed.reshape(step_count, seq_rows, width_q).astype(jnp.bfloat16)


def on_device(tokens, norm_gain, w_qkv, w_out, cache_k, cache_v, lengths):
    gathered = lax.all_gather(tokens, "wide", axis=2, tiled=True)
    widened = gathered.astype(jnp.float32)
    center = jnp.mean(widened, axis=-1, keepdims=True)
    spread = jnp.mean(widened * widened, axis=-1, keepdims=True) - center * center
    normed = ((widened - center) * lax.rsqrt(spread + norm_eps) * norm_gain).astype(jnp.bfloat16)
    projected = jnp.einsum("sbd,dc->sbc", normed, w_qkv, preferred_element_type=jnp.float32)
    projected = projected.astype(jnp.bfloat16)
    per_sequence = lax.all_to_all(projected, "wide", split_axis=1, concat_axis=2, tiled=True)
    head_dim = cache_k.shape[2]
    heads = per_sequence.shape[2] // head_dim - 2
    mixed = attend(per_sequence, cache_k, cache_v, lengths, heads, head_dim)
    result = jnp.einsum(
        "snh,hd->snd",
        lax.all_gather(mixed, "wide", axis=1, tiled=True),
        w_out,
        preferred_element_type=jnp.float32,
    )
    return result.astype(jnp.bfloat16)


def iota(shape, axis):
    return lax.broadcasted_iota(jnp.int32, shape, axis)


def pick(mask):
    return jnp.where(mask, 1.0, 0.0).astype(jnp.bfloat16)


def dot(a, b):
    return jnp.dot(a, b, preferred_element_type=jnp.float32)


def dot_t(a, b):
    return lax.dot_general(a, b, (((1,), (1,)), ((), ())), preferred_element_type=jnp.float32)


def fused_kernel(
    lengths,
    tokens,
    gain,
    w_qkv,
    w_out,
    cache_k,
    cache_v,
    out,
    shards,
    stats,
    w_in,
    w_last,
    keys,
    values,
    acc,
    to_send,
    arrived,
    gathered,
    total,
    columns,
    local_sem,
    last_sem,
    cache_sem,
    stat_send,
    stat_recv,
    send1,
    recv1,
    near1,
    all_send,
    all_recv,
    send2,
    recv2,
    near2,
    angles,
):
    me = lax.axis_index("wide")
    z = me // (Y * C)
    y = (me // C) % Y
    c = me % C
    depth = tokens.shape[1]
    rows = tokens.shape[0]
    seqs = rows // 2
    out_depth = w_last.shape[1]
    width = w_qkv.shape[0]
    heads = w_out.shape[0] // 256
    groups = heads // GROUP
    mirrored = (z + z // 2) % 2
    upper = z // 2

    def z_at(p):
        m = p + mirrored * (1 - 2 * p) * (1 - p // 2)
        return m + upper * (3 - 2 * m)

    def index(zz, yy, cc):
        return (zz * Y + yy) * C + cc

    def remote(src, dst, send_sem, recv_sem, target):
        return pltpu.make_async_remote_copy(
            src_ref=src,
            dst_ref=dst,
            send_sem=send_sem,
            recv_sem=recv_sem,
            device_id={"wide": target},
            device_id_type=MESH,
        )

    y_peer = index(z, 1 - y, c)
    c_peer = index(z, y, 1 - c)

    def next_z(zz):
        return z + jnp.where(zz > z, -1, 1)

    def can_go(zz):
        after = next_z(zz)
        return jnp.logical_and(after >= 0, after < Z)

    def send_own(copy, h):
        @pl.when(z < Z - 1)
        def _():
            copy(me, h, 0, index(z + 1, y, c)).start()

        @pl.when(z > 0)
        def _():
            copy(me, h, 0, index(z - 1, y, c)).start()

        copy(me, h, 1, y_peer).start()
        copy(me, h, 2, c_peer).start()

    def pass_on(copy, h, p):
        zz = z_at(p)
        owner = index(zz, y, c)
        copy(owner, h, 0, c_peer).wait_recv()

        @pl.when(can_go(zz))
        def _():
            copy(owner, h, 0, index(next_z(zz), y, c)).start()

        copy(owner, h, 1, y_peer).start()
        copy(owner, h, 2, c_peer).start()

    def pass_y(copy, h, p):
        owner = index(z_at(p), 1 - y, c)
        copy(owner, h, 1, c_peer).wait_recv()
        copy(owner, h, 2, c_peer).start()

    def all_sent(buffer, sems):
        def sent(count, kind):
            part = buffer.at[pl.ds(0, count)]
            remote(part, part, sems.at[kind], sems.at[kind], c_peer).wait_send()

        @pl.when(mirrored == 1)
        def _():
            sent(5, 0)

        @pl.when(mirrored == 0)
        def _():
            sent(1, 0)

        sent(4, 1)
        sent(8, 2)

    def load_in(owner):
        return pltpu.make_async_copy(
            w_qkv.at[:, pl.ds(pl.multiple_of(owner * depth, depth), depth)],
            w_in.at[owner],
            local_sem.at[owner],
        )

    def load_last(g):
        return pltpu.make_async_copy(
            w_out.at[pl.ds(pl.multiple_of(g * out_depth, out_depth), out_depth)],
            w_last.at[g % SLOTS],
            last_sem.at[g],
        )

    load_keys = pltpu.make_async_copy(cache_k, keys, cache_sem.at[0])
    load_values = pltpu.make_async_copy(cache_v, values, cache_sem.at[1])

    def load_round(p, carry):
        @pl.when(p <= 3)
        def _():
            load_in(index(z_at(p), y, c)).start()
            load_in(index(z_at(p), y, 1 - c)).start()

        @pl.when(p >= 1)
        def _():
            load_in(index(z_at(p - 1), 1 - y, c)).start()
            load_in(index(z_at(p - 1), 1 - y, 1 - c)).start()

        return carry

    lax.fori_loop(0, 5, load_round, 0)

    barrier = pltpu.get_barrier_semaphore()

    def greet(k, carry):
        pl.semaphore_signal(
            barrier, inc=1, device_id={"wide": (me + k) % WIDE}, device_id_type=MESH
        )
        return carry

    lax.fori_loop(1, WIDE, greet, 0)

    widened = tokens[...].astype(jnp.float32)
    diagonal = iota((rows, 128), 0) == iota((rows, 128), 1)

    def as_row(column):
        return jnp.sum(jnp.where(diagonal, column, 0.0), axis=0, keepdims=True)

    def as_column(row):
        return jnp.sum(jnp.where(diagonal, row, 0.0), axis=1, keepdims=True)

    sums = as_row(jnp.sum(widened, axis=1, keepdims=True))
    squares = as_row(jnp.sum(widened * widened, axis=1, keepdims=True))
    line = iota((8, 128), 0)
    stats[me] = jnp.where(line == 0, sums, jnp.where(line == 1, squares, 0.0))

    pl.semaphore_wait(barrier, WIDE - 1)

    def stat_copy(k):
        return remote(
            stats.at[me], stats.at[me], stat_send.at[0], stat_recv.at[0], (me + k) % WIDE
        )

    def stat_start(k, carry):
        stat_copy(k).start()
        return carry

    lax.fori_loop(1, WIDE, stat_start, 0)

    share = rows // HALVES

    def into(owner, h, k):
        return near1.at[owner] if k == 2 else recv1.at[h, owner]

    def shard_copy(owner, h, k, target):
        part = shards.at[owner, pl.ds(pl.multiple_of(h * share, share), share)]
        return remote(part, part, send1.at[k], into(owner, h, k), target)

    def own_copy(owner, h, k, target):
        part = tokens.at[pl.ds(pl.multiple_of(h * share, share), share)]
        there = shards.at[me, pl.ds(pl.multiple_of(h * share, share), share)]
        return remote(part, there, send1.at[k], into(me, h, k), target)

    def own_start(h, carry):
        send_own(own_copy, h)
        return carry

    lax.fori_loop(0, HALVES, own_start, 0)

    freqs = jnp.exp(iota((8, 128), 1).astype(jnp.float32) * (-2.0 * math.log(10000.0) / 256))
    line = iota((8, 128), 0)
    position = jnp.where((line & 1) == 0, lengths[0], lengths[1]) + ((line >> 1) & 1)
    angle = position.astype(jnp.float32) * freqs
    angles[0] = jnp.cos(angle)
    angles[1] = jnp.sin(angle)
    shards[me] = tokens[...]
    acc[...] = jnp.zeros_like(acc)

    others = stats.at[pl.ds(0, WIDE - 1)]

    def settle():
        remote(others, others, stat_send.at[0], stat_recv.at[0], c_peer).wait_recv()
        whole = jnp.sum(stats[...], axis=0)
        features = float(depth * WIDE)
        center = as_column(whole[0:1]) / features
        spread = as_column(whole[1:2]) / features - center * center
        columns[0] = jnp.broadcast_to(center, (rows, 128))
        columns[1] = jnp.broadcast_to(lax.rsqrt(spread + norm_eps), (rows, 128))

    def project(owner):
        load_in(owner).wait()
        x = shards[owner].astype(jnp.float32)
        normed = (x - columns[0][:, 0:1]) * columns[1][:, 0:1] * gain[owner]
        acc[:, 0:width] += dot_t(normed.astype(jnp.bfloat16), w_in[owner])

    def round1(p, carry):
        @pl.when(p == 2)
        def _():
            load_keys.start()
            load_values.start()

            def body(g, inner):
                load_last(g).start()
                return inner

            lax.fori_loop(0, SLOTS, body, 0)

        def part(i, inner):
            @pl.when(jnp.logical_and(p >= 1, p <= 3))
            def _():
                pass_on(shard_copy, i, p)

            @pl.when(jnp.logical_and(p >= 1, p <= 4))
            def _():
                pass_y(shard_copy, i, p - 1)

            @pl.when(jnp.logical_and(p == 1, i == 0))
            def _():
                settle()

            late = 1 + i // 2

            @pl.when(jnp.logical_and(p - late >= 0, p - late <= 3))
            def _():
                owner = index(z_at(p - late), (y + i // 2) % Y, (c + i) % C)

                @pl.when(i % 2 == 1)
                def _():
                    whole_shard = shards.at[owner]
                    remote(
                        whole_shard, whole_shard, send1.at[2], near1.at[owner], c_peer
                    ).wait_recv()

                project(owner)

            return inner

        return lax.fori_loop(0, HALVES, part, carry)

    lax.fori_loop(0, 6, round1, 0)

    offset = (width * me) % 256
    shifted = pltpu.roll(acc[...], offset, 1).astype(jnp.bfloat16)
    row = iota((WIDE * 16, rows), 0)
    token = ((row >> 1) & 1) * seqs + 2 * (row >> 4) + (row & 1)
    chosen = iota((WIDE * 16, rows), 1) == token
    sending = jnp.zeros((WIDE * 16, 256), jnp.float32)
    for hh in range(GROUP):
        sending += dot(
            pick(jnp.logical_and(chosen, ((row >> 2) & 3) == hh)),
            shifted[:, hh * 256 : (hh + 1) * 256],
        )
    to_send[...] = sending.astype(jnp.bfloat16).reshape(to_send.shape)

    def all_copy(k):
        t = (me + k) % WIDE
        return remote(to_send.at[t], arrived.at[me], all_send.at[0], all_recv.at[0], t)

    def all_start(k, carry):
        all_copy(k).start()
        return carry

    lax.fori_loop(1, WIDE, all_start, 0)
    arrived[me] = to_send[me]
    load_keys.wait()
    load_values.wait()

    received = arrived.at[pl.ds(0, WIDE - 1)]
    remote(received, received, all_send.at[0], all_recv.at[0], c_peer).wait_recv()

    blocks = arrived[...].reshape(WIDE * 16, 256)
    query_rows = 2 * heads
    col = iota((query_rows + 16, WIDE * 16), 1)
    head = ((width * (col >> 4)) >> 8) + ((col >> 2) & 3)
    step = (col >> 1) & 1
    target = jnp.where(
        head < heads, step * heads + head, query_rows + 8 * (head - heads) + step
    )
    placed = iota((query_rows + 16, WIDE * 16), 0) == target
    scale = 1.0 / math.sqrt(256)
    slots = keys.shape[1]
    sending = jnp.zeros((4 * heads, 256), jnp.float32)
    for n in range(2):
        mine = dot(pick(jnp.logical_and(placed, (col & 1) == n)), blocks)

        def turn(block, cosine, sine_table):
            first, second = block[:, 0:128], block[:, 128:256]
            return jnp.concatenate(
                [first * cosine - second * sine_table, second * cosine + first * sine_table],
                axis=1,
            ).astype(jnp.bfloat16)

        def by_step(table, count, half):
            at = iota((count, 128), 0)
            return jnp.where(at < half, table[n : n + 1, :], table[n + 2 : n + 3, :])

        query = turn(
            mine[0:query_rows],
            by_step(angles[0], query_rows, heads),
            by_step(angles[1], query_rows, heads),
        )
        key_new = turn(
            mine[query_rows : query_rows + 8], by_step(angles[0], 8, 1), by_step(angles[1], 8, 1)
        )
        value_new = mine[query_rows + 8 : query_rows + 16].astype(jnp.bfloat16)
        scores = dot_t(query, keys[n]) * scale
        scores = jnp.where(iota((query_rows, slots), 1) < lengths[n], scores, -1e30)
        fresh = dot_t(query, key_new) * scale
        t = iota((query_rows, 8), 1)
        s = jnp.where(iota((query_rows, 8), 0) >= heads, 1, 0)
        fresh = jnp.where(t <= s, fresh, -1e30)
        top = jnp.maximum(
            jnp.max(scores, axis=1, keepdims=True), jnp.max(fresh, axis=1, keepdims=True)
        )
        scores = jnp.exp(scores - top)
        fresh = jnp.exp(fresh - top)
        denom = jnp.sum(scores, axis=1, keepdims=True) + jnp.sum(fresh, axis=1, keepdims=True)
        inverse = 1.0 / denom
        mixed = dot((scores * inverse).astype(jnp.bfloat16), values[n])
        mixed += dot((fresh * inverse).astype(jnp.bfloat16), value_new)
        at = iota((4 * heads, query_rows), 0)
        from_row = ((at >> 1) & 1) * heads + (at >> 2)
        sending += dot(
            pick(
                jnp.logical_and(
                    iota((4 * heads, query_rows), 1) == from_row, (at & 1) == n
                )
            ),
            mixed.astype(jnp.bfloat16),
        )
    gathered[me] = sending.astype(jnp.bfloat16)

    high = gathered.shape[1] // PIECES

    def piece_copy(owner, q, k, target):
        part = gathered.at[owner, pl.ds(pl.multiple_of(q * high, high), high)]
        arrives = near2.at[q] if k == 2 else recv2.at[q, owner]
        return remote(part, part, send2.at[k], arrives, target)

    def piece_start(q, carry):
        send_own(piece_copy, q)
        return carry

    lax.fori_loop(0, PIECES, piece_start, 0)

    def pass_round(p, carry):
        def body(q, inner):
            pass_on(piece_copy, q, p)
            pass_y(piece_copy, q, p - 1)
            return inner

        return lax.fori_loop(0, PIECES, body, carry)

    lax.fori_loop(1, Z, pass_round, 0)

    def stage_c(q):
        part = gathered.at[pl.ds(0, WIDE // 2), pl.ds(0, high)]
        remote(part, part, send2.at[2], near2.at[q], c_peer).wait_recv()

    total[...] = jnp.zeros_like(total)
    per_piece = groups // PIECES
    i = iota((rows * GROUP, WIDE * 16), 0)
    m = i % rows
    b = m % seqs
    source = (b >> 1) * 16 + (i // rows) * 4 + (m // seqs) * 2 + (b & 1)
    reorder = pick(iota((rows * GROUP, WIDE * 16), 1) == source)

    def multiply(g, carry):
        @pl.when(g % per_piece == 0)
        def _():
            q = g // per_piece

            @pl.when(q < PIECES - 1)
            def _():
                pass_y(piece_copy, q + 1, 3)

            stage_c(q)

        load_last(g).wait()
        block = gathered[:, pl.ds(pl.multiple_of(g * 16, 16), 16), :].reshape(WIDE * 16, 256)
        ordered = dot(reorder, block).astype(jnp.bfloat16)
        lined = jnp.concatenate(
            [ordered[h * rows : (h + 1) * rows] for h in range(GROUP)], axis=1
        )
        total[...] += dot(lined, w_last[g % SLOTS])

        @pl.when(g + SLOTS < groups)
        def _():
            load_last(g + SLOTS).start()

        return carry

    pass_y(piece_copy, 0, 3)
    lax.fori_loop(0, groups, multiply, 0)
    out[...] = total[...].astype(jnp.bfloat16)

    remote(others, others, stat_send.at[0], stat_recv.at[0], c_peer).wait_send()
    left = to_send.at[pl.ds(0, WIDE - 1)]
    remote(left, left, all_send.at[0], all_recv.at[0], c_peer).wait_send()
    all_sent(shards, send1)
    all_sent(gathered, send2)


def fused(tokens, norm_gain, w_qkv, w_out, cache_k, cache_v, lengths):
    step_count, seqs, depth = tokens.shape
    rows = step_count * seqs
    inner, out_width = w_out.shape
    head_dim = cache_k.shape[2]
    heads = inner // head_dim
    vmem = pl.BlockSpec(memory_space=pltpu.VMEM)
    anywhere = pl.BlockSpec(memory_space=pl.ANY)
    dma = pltpu.SemaphoreType.DMA
    result = pl.pallas_call(
        fused_kernel,
        out_shape=jax.ShapeDtypeStruct((rows, out_width), jnp.bfloat16),
        in_specs=[pl.BlockSpec(memory_space=pltpu.SMEM)] + [vmem] * 2 + [anywhere] * 4,
        out_specs=vmem,
        scratch_shapes=[
            pltpu.VMEM((WIDE, rows, depth), jnp.bfloat16),
            pltpu.VMEM((WIDE, 8, 128), jnp.float32),
            pltpu.VMEM((WIDE, w_qkv.shape[1], depth), jnp.bfloat16),
            pltpu.VMEM((SLOTS, GROUP * head_dim, out_width), jnp.bfloat16),
            pltpu.VMEM(cache_k.shape, jnp.bfloat16),
            pltpu.VMEM(cache_v.shape, jnp.bfloat16),
            pltpu.VMEM((rows, GROUP * head_dim), jnp.float32),
            pltpu.VMEM((WIDE, 16, head_dim), jnp.bfloat16),
            pltpu.VMEM((WIDE, 16, head_dim), jnp.bfloat16),
            pltpu.VMEM((WIDE, 4 * heads, head_dim), jnp.bfloat16),
            pltpu.VMEM((rows, out_width), jnp.float32),
            pltpu.VMEM((2, rows, 128), jnp.float32),
            dma((WIDE,)),
            dma((heads // GROUP,)),
            dma((2,)),
            dma((1,)),
            dma((1,)),
            dma((3,)),
            dma((HALVES, WIDE)),
            dma((WIDE,)),
            dma((1,)),
            dma((1,)),
            dma((3,)),
            dma((PIECES, WIDE)),
            dma((PIECES,)),
            pltpu.VMEM((2, 8, 128), jnp.float32),
        ],
        compiler_params=pltpu.CompilerParams(
            collective_id=0, has_side_effects=True, vmem_limit_bytes=62 * 1024 * 1024
        ),
    )(
        lengths,
        tokens.reshape(rows, depth),
        norm_gain.reshape(WIDE, 1, depth),
        w_qkv.T,
        w_out,
        cache_k,
        cache_v,
    )
    return result.reshape(step_count, seqs, out_width)


def solution(mesh):
    placed = (
        P(None, "groups", "wide"),
        P(),
        P(None, "wide"),
        P(None, "wide"),
        P(("groups", "wide"), None, None),
        P(("groups", "wide"), None, None),
        P(("groups", "wide")),
    )
    return jax.shard_map(
        fused if mesh.shape["wide"] == WIDE else on_device, mesh=mesh, in_specs=placed, out_specs=P(None, "groups", "wide"), check_vma=False
    )
```
